512 devices in a mesh: ctx: 32 (over z_lo, x, core), ch: 16 (over z_hi, y).
Axes of the slice: x: 4, y: 4, z: 16 (z_hi: 4, z_lo: 4; z = z_hi * 4 + z_lo), core: 2. Of those that a mesh axis runs over, the one named last changes fastest.
Arguments:
- proj: bfloat16 [3, 4096, 8192], P(None, 'ch', 'ctx'), may hold values from -6 to 6
- short_filter: float32 [3, 4096, 3], P(None, 'ch'), may hold values from -3 to 3
- residues: float32 [4096, 16], P('ch'), may hold values from -1.8 to 1.8
- decays: float32 [4096, 16], P('ch'), may hold values from 6.1035156e-05 to 0.03
- skip: float32 [4096], P('ch'), may hold values from -1 to 1
- w_out: bfloat16 [4096, 4096], P(None, 'ch'), may hold values from -0.09375 to 0.09375
Outputs:
- mixed_out: bfloat16 [8192, 4096], P('ctx', 'ch')
The draws below stay inside these ranges and needn't reach their ends.
All inputs are finite; a program needn't handle non-finite values.
Results may differ from the reference program's by a relative error of at most 0.015.
Values may be sent and summed in bfloat16 or wider, within the bound.
No kernel may reach another device: no remote copies, remote signals or barrier semaphores. Data moves between devices by JAX's collectives and lax.ppermute only.
A program may use at most 192 MiB of HBM per device.

```python
import math
import jax
import jax.numpy as jnp
from jax import lax

D = 4096
MODES = 16
SEQ = 8192


def shard_levels(key, dims, pieces, smallest, high):
    level = 1.0
    for axis_at, blocks in pieces:
        heights = jax.random.uniform(jax.random.fold_in(jax.random.fold_in(key, 6), axis_at), (blocks,), jnp.float32, smallest / len(pieces), high / len(pieces))
        level = level * jnp.repeat(jnp.exp(heights), dims[axis_at] // blocks).reshape((-1,) + (1,) * (len(dims) - 1 - axis_at))
    return level


def scatter_about(rng, shape, scale, limit, split=(), kind=jnp.bfloat16):
    factor_of = shard_levels(rng, shape, split, -0.22, 0.18) if split else 1.0
    drawn = jax.random.normal(rng, shape, jnp.float32) * scale * factor_of
    return jnp.minimum(jnp.maximum(drawn, -limit), limit).astype(kind)


def setup_inputs(seed: int = 0) -> dict:
    arg_keys = jax.random.split(jax.random.key(seed), 7)
    return {
        "proj": scatter_about(arg_keys[0], (3, D, SEQ), 1.0, 6.0, ((1, 16), (2, 32))),
        "short_filter": scatter_about(arg_keys[1], (3, D, 3), 0.6, 3.0, ((1, 16),), jnp.float32),
        "residues": scatter_about(arg_keys[2], (D, MODES), 0.3, 1.8, ((0, 16),), jnp.float32),
        "decays": jnp.clip(jnp.exp(math.log(0.03) - 6.1975026 * jax.random.uniform(arg_keys[3], (D, MODES), jnp.float32) ** shard_levels(arg_keys[3], (D, MODES), ((0, 16),), -0.2, 0.2)), 6.103515625e-05, 0.03),
        "skip": jnp.clip(jax.random.uniform(arg_keys[4], (D,), jnp.float32, -1.0, 1.0) * shard_levels(arg_keys[4], (D,), ((0, 16),), -0.4, 0.0), -1.0, 1.0),
        "w_out": scatter_about(arg_keys[5], (D, D), D ** -0.5, 0.09375, ((1, 16),)),
    }


def filter_taps(mode_gain, mode_rate, length):
    positions = jnp.arange(length, dtype=jnp.int32).astype(jnp.float32)

    def add_mode(mode, running):
        one_gain = lax.dynamic_slice_in_dim(mode_gain, mode, 1, 1)
        one_rate = lax.dynamic_slice_in_dim(mode_rate, mode, 1, 1)
        return running + one_gain * jnp.exp(-one_rate * positions[None, :])
    initial = jnp.zeros((mode_gain.shape[0], length), jnp.float32)
    return lax.fori_loop(0, mode_gain.shape[1], add_mode, initial)

def reference(proj, short_filter, residues, decays, skip, w_out):
    inputs = proj.astype(jnp.float32)
    padded = jnp.pad(inputs, ((0, 0), (0, 0), (2, 0)))
    shortmix = short_filter[:, :, 0:1] * inputs + short_filter[:, :, 1:2] * padded[:, :, 1:-1] + short_filter[:, :, 2:3] * padded[:, :, :-2]
    query = shortmix[0].astype(jnp.bfloat16)
    signal = (shortmix[1] * shortmix[2]).astype(jnp.bfloat16)
    mode_gain = residues * jnp.sqrt(-jnp.expm1(-2.0 * decays))
    width, length = signal.shape
    block = math.gcd(width, 256)
    count = width // block
    extent = 2 * length

    def one_block(operands):
        signal_block, gain_block, rate_block = operands
        taps = filter_taps(gain_block, rate_block, length)
        spectrum = jnp.fft.rfft(signal_block.astype(jnp.float32), n=extent, axis=1) * jnp.fft.rfft(taps, n=extent, axis=1)
        return jnp.fft.irfft(spectrum, n=extent, axis=1)[:, :length].astype(jnp.float32)
    longconv = lax.map(one_block, (signal.reshape(count, block, length), mode_gain.reshape(count, block, MODES), decays.reshape(count, block, MODES)))
    longconv = longconv.reshape(width, length)
    longconv = lax.optimization_barrier(longconv.astype(jnp.bfloat16)).astype(jnp.float32)
    gated = (query.astype(jnp.float32) * (longconv + skip[:, None] * signal.astype(jnp.float32))).astype(jnp.bfloat16)
    return jnp.dot(gated.T, w_out, preferred_element_type=jnp.float32).astype(jnp.bfloat16)
```

```python
import functools

import jax
import jax.numpy as jnp
from jax import lax
from jax.experimental import pallas as pl
from jax.experimental.pallas import tpu as pltpu
from jax.sharding import PartitionSpec as P

F32 = jnp.float32
BF16 = jnp.bfloat16
LANES = 128
SUB = 8
VMEM_LIMIT = 48 * 1024 * 1024


def pallas(body, out_shape, scratch=(), **kwargs):
    return pl.pallas_call(
        body,
        out_shape=out_shape,
        scratch_shapes=list(scratch),
        compiler_params=pltpu.CompilerParams(vmem_limit_bytes=VMEM_LIMIT),
        **kwargs,
    )


def edge_kernel(proj_ref, edge_ref):
    rows = [proj_ref[i].astype(F32).T[-2:, :] for i in range(3)]
    rows.append(jnp.zeros((2, proj_ref.shape[1]), F32))
    edge_ref[...] = jnp.concatenate(rows, axis=0).astype(BF16)


def halves(width):
    return [slice(lo, lo + LANES) for lo in range(0, width, LANES)]


def state_kernel(
    proj_ref, halo_ref, filter_ref, decay_ref,
    signal_ref, query_ref, ends_ref, state_ref,
    line_ref, coef_ref, sums_ref,
):
    width, length = proj_ref.shape[1:]
    steps = length // SUB
    modes = decay_ref.shape[1]
    decay = decay_ref[...].T
    coef_ref[...] = decay
    halo = halo_ref[...].astype(F32)
    for i in range(3):
        block = proj_ref[i].astype(F32).T
        for h, cols in enumerate(halves(width)):
            line_ref[i, h, SUB - 2 : SUB, :] = halo[2 * i : 2 * i + 2, cols]
            line_ref[i, h, SUB:, :] = block[:, cols]
    taps = [filter_ref[i].T for i in range(3)]
    chunk_id = lax.broadcasted_iota(jnp.int32, (SUB, LANES), 0).astype(F32)
    for h, cols in enumerate(halves(width)):
        tap = [[jnp.broadcast_to(taps[i][m : m + 1, cols], (SUB, LANES)) for m in range(3)] for i in range(3)]
        rate = [jnp.broadcast_to(coef_ref[m : m + 1, cols], (SUB, LANES)) for m in range(modes)]
        keep = [jnp.exp(-r) for r in rate]
        state = [jnp.zeros((SUB, LANES), F32) for _ in range(modes)]

        def rows(i, at):
            return line_ref[i, h, pl.ds(SUB + at, SUB, stride=steps), :]

        back2 = [rows(i, -2) for i in range(3)]
        back1 = [rows(i, -1) for i in range(3)]
        for p in range(steps):
            here = [rows(i, p) for i in range(3)]
            mix = [tap[i][0] * here[i] + tap[i][1] * back1[i] + tap[i][2] * back2[i] for i in range(3)]
            back2, back1 = back1, here
            signal = (mix[1] * mix[2]).astype(BF16).astype(F32)
            signal_ref[p, :, cols] = signal
            query_ref[p, :, cols] = mix[0].astype(BF16).astype(F32)
            state = [keep[m] * state[m] + signal for m in range(modes)]
        for m in range(modes):
            ends_ref[m, :, cols] = state[m]
            weight = jnp.exp(-rate[m] * (float(steps) * (SUB - 1 - chunk_id)))
            sums_ref[m : m + 1, cols] = jnp.sum(weight * state[m], axis=0, keepdims=True)
    sent = sums_ref[...].astype(BF16)
    for j in range(state_ref.shape[0]):
        state_ref[j] = sent


def gate_kernel(
    place_ref, given_ref, signal_ref, query_ref, ends_ref, decay_ref, residue_ref, skip_ref,
    gated_ref,
    carry_ref, gain_ref, coef_ref, line_ref,
):
    blocks, modes, width = given_ref.shape
    steps = signal_ref.shape[0]
    length = steps * SUB
    place = place_ref[0]
    decay = decay_ref[...].T
    coef_ref[...] = decay
    twice = 2.0 * decay
    series = jnp.ones_like(twice)
    for n in (8, 7, 6, 5, 4, 3, 2):
        series = 1.0 - twice * (1.0 / n) * series
    gain_ref[...] = residue_ref[...].T * jnp.sqrt(twice * series)
    per_block = jnp.exp(-float(length) * decay)
    carry = jnp.zeros_like(decay)
    for j in range(blocks - 1):
        carry = jnp.where(j < place, per_block * carry + given_ref[j].astype(F32), carry)
    carry_ref[...] = carry
    chunk_id = lax.broadcasted_iota(jnp.int32, (SUB, LANES), 0)
    for h, cols in enumerate(halves(width)):
        rate = [jnp.broadcast_to(coef_ref[m : m + 1, cols], (SUB, LANES)) for m in range(modes)]
        state = []
        for m in range(modes):
            enters = jnp.broadcast_to(carry_ref[m : m + 1, cols], (SUB, LANES))
            run = jnp.where(chunk_id == 0, enters, pltpu.roll(ends_ref[m, :, cols], 1, 0))
            for far in (1, 2, 4):
                moved = jnp.where(chunk_id >= far, pltpu.roll(run, far, 0), 0.0)
                run = run + jnp.exp(-float(steps * far) * rate[m]) * moved
            state.append(run)
        keep = [jnp.exp(-r) for r in rate]
        gain = [jnp.broadcast_to(gain_ref[m : m + 1, cols], (SUB, LANES)) for m in range(modes)]
        skip = jnp.broadcast_to(skip_ref[0:1, cols], (SUB, LANES))
        for p in range(steps):
            signal = signal_ref[p, :, cols]
            state = [keep[m] * state[m] + signal for m in range(modes)]
            terms = [gain[m] * state[m] for m in range(modes)]
            while len(terms) > 1:
                terms = [a + b for a, b in zip(terms[::2], terms[1::2])]
            conv = terms[0].astype(BF16).astype(F32)
            line_ref[h, pl.ds(p, SUB, stride=steps), :] = query_ref[p, :, cols] * (conv + skip * signal)
        gated_ref[:, cols] = line_ref[h].astype(BF16)


def mix_kernel(gated_ref, w_ref, out_ref, total_ref):
    step = pl.program_id(0)
    part = sum(
        jnp.dot(gated_ref[0, k], w_ref[k, 0], preferred_element_type=F32)
        for k in range(gated_ref.shape[1])
    )

    @pl.when(step == 0)
    def _():
        total_ref[...] = part

    @pl.when(step > 0)
    def _():
        total_ref[...] += part

    @pl.when(step == pl.num_programs(0) - 1)
    def _():
        out_ref[...] = total_ref[...].astype(BF16)


def per_device(outer, proj, short_filter, residues, decays, skip, w_out):
    _, width, length = proj.shape
    modes = decays.shape[1]
    blocks = lax.axis_size("ctx")
    groups = lax.axis_size("ch")
    inner = groups // outer
    steps = length // SUB
    shape = jax.ShapeDtypeStruct

    edge = pl.pallas_call(
        edge_kernel,
        grid=(1,),
        in_specs=[pl.BlockSpec((3, width, LANES), lambda i: (0, 0, length // LANES - 1))],
        out_specs=pl.BlockSpec((SUB, width), lambda i: (0, 0)),
        out_shape=shape((SUB, width), BF16),
    )(proj)
    halo = lax.ppermute(edge, "ctx", [(i, i + 1) for i in range(blocks - 1)])
    signal, query, ends, state = pallas(
        state_kernel,
        (
            shape((steps, SUB, width), F32),
            shape((steps, SUB, width), F32),
            shape((modes, SUB, width), F32),
            shape((blocks, modes, width), BF16),
        ),
        (
            pltpu.VMEM((3, width // LANES, SUB + length, LANES), F32),
            pltpu.VMEM((modes, width), F32),
            pltpu.VMEM((modes, width), F32),
        ),
    )(proj, halo, short_filter, decays)
    given = lax.all_to_all(state, "ctx", 0, 0)
    place = lax.axis_index("ctx").astype(jnp.int32).reshape(1)
    whole = pl.BlockSpec(memory_space=pltpu.VMEM)
    gated = pallas(
        gate_kernel,
        shape((length, width), BF16),
        (
            pltpu.VMEM((modes, width), F32),
            pltpu.VMEM((modes, width), F32),
            pltpu.VMEM((modes, width), F32),
            pltpu.VMEM((width // LANES, length, LANES), F32),
        ),
        in_specs=[pl.BlockSpec(memory_space=pltpu.SMEM)] + [whole] * 7,
    )(place, given, signal, query, ends, decays, residues, skip.reshape(1, width))
    along_outer = [[a * inner + b for a in range(outer)] for b in range(inner)]
    along_inner = [[a * inner + b for b in range(inner)] for a in range(outer)]
    near = lax.all_gather(gated, "ch", axis_index_groups=along_outer)
    full = lax.all_gather(near, "ch", axis_index_groups=along_inner)
    return pl.pallas_call(
        mix_kernel,
        grid=(inner,),
        in_specs=[
            pl.BlockSpec((1, outer, length, width), lambda i: (i, 0, 0, 0)),
            pl.BlockSpec((outer, 1, width, w_out.shape[1]), lambda i: (0, i, 0, 0)),
        ],
        out_specs=pl.BlockSpec((length, w_out.shape[1]), lambda i: (0, 0)),
        out_shape=shape((length, w_out.shape[1]), BF16),
        scratch_shapes=[pltpu.VMEM((length, w_out.shape[1]), F32)],
        compiler_params=pltpu.CompilerParams(vmem_limit_bytes=VMEM_LIMIT),
    )(full, w_out.reshape(outer, inner, width, w_out.shape[1]))


def solution(mesh):
    groups = mesh.shape["ch"]
    outer = 4 if groups % 4 == 0 else 1
    in_specs = (
        P(None, "ch", "ctx"),
        P(None, "ch", None),
        P("ch", None),
        P("ch", None),
        P("ch"),
        P(None, "ch"),
    )
    return jax.shard_map(
        functools.partial(per_device, outer),
        mesh=mesh,
        in_specs=in_specs,
        out_specs=P("ctx", "ch"),
        check_vma=False,
    )
```

```python
import functools

import jax
import jax.numpy as jnp
from jax import lax
from jax.experimental import pallas as pl
from jax.experimental.pallas import tpu as pltpu
from jax.sharding import PartitionSpec as P

F32 = jnp.float32
BF16 = jnp.bfloat16
LANES = 128
SUB = 8
VMEM_LIMIT = 48 * 1024 * 1024


def pallas(body, out_shape, scratch=(), **kwargs):
    return pl.pallas_call(
        body,
        out_shape=out_shape,
        scratch_shapes=list(scratch),
        compiler_params=pltpu.CompilerParams(vmem_limit_bytes=VMEM_LIMIT),
        **kwargs,
    )


def edge_kernel(proj_ref, edge_ref):
    rows = [proj_ref[i].astype(F32).T[-2:, :] for i in range(3)]
    rows.append(jnp.zeros((2, proj_ref.shape[1]), F32))
    edge_ref[...] = jnp.concatenate(rows, axis=0).astype(BF16)


def halves(width):
    return [slice(lo, lo + LANES) for lo in range(0, width, LANES)]


def state_kernel(
    proj_ref, halo_ref, filter_ref, decay_ref,
    signal_ref, query_ref, ends_ref, state_ref,
    line_ref, sums_ref,
):
    width, length = proj_ref.shape[1:]
    steps = length // SUB
    modes = decay_ref.shape[0]
    halo = halo_ref[...].astype(F32)
    for i in range(3):
        block = proj_ref[i].astype(F32).T
        for h, cols in enumerate(halves(width)):
            line_ref[i, h, SUB - 2 : SUB, :] = halo[2 * i : 2 * i + 2, cols]
            line_ref[i, h, SUB:, :] = block[:, cols]
    chunk_id = lax.broadcasted_iota(jnp.int32, (SUB, LANES), 0).astype(F32)
    for h, cols in enumerate(halves(width)):
        tap = [[jnp.broadcast_to(filter_ref[i, m : m + 1, cols], (SUB, LANES)) for m in range(3)] for i in range(3)]
        rate = [jnp.broadcast_to(decay_ref[m : m + 1, cols], (SUB, LANES)) for m in range(modes)]
        keep = [jnp.exp(-r) for r in rate]
        state = [jnp.zeros((SUB, LANES), F32) for _ in range(modes)]

        def rows(i, at):
            return line_ref[i, h, pl.ds(SUB + at, SUB, stride=steps), :]

        back2 = [rows(i, -2) for i in range(3)]
        back1 = [rows(i, -1) for i in range(3)]
        for p in range(steps):
            here = [rows(i, p) for i in range(3)]
            mix = [tap[i][0] * here[i] + tap[i][1] * back1[i] + tap[i][2] * back2[i] for i in range(3)]
            back2, back1 = back1, here
            signal = (mix[1] * mix[2]).astype(BF16).astype(F32)
            signal_ref[p, :, cols] = signal
            query_ref[p, :, cols] = mix[0].astype(BF16).astype(F32)
            state = [keep[m] * state[m] + signal for m in range(modes)]
        for m in range(modes):
            ends_ref[m, :, cols] = state[m]
            weight = jnp.exp(-rate[m] * (float(steps) * (SUB - 1 - chunk_id)))
            sums_ref[m : m + 1, cols] = jnp.sum(weight * state[m], axis=0, keepdims=True)
    sent = sums_ref[...].astype(BF16)
    for j in range(state_ref.shape[0]):
        state_ref[j] = sent


def gate_kernel(
    place_ref, given_ref, signal_ref, query_ref, ends_ref, decay_ref, residue_ref, skip_ref,
    gated_ref,
    carry_ref, gain_ref, line_ref,
):
    blocks, modes, width = given_ref.shape
    steps = signal_ref.shape[0]
    length = steps * SUB
    place = place_ref[0]
    decay = decay_ref[...]
    twice = 2.0 * decay
    series = jnp.ones_like(twice)
    for n in (8, 7, 6, 5, 4, 3, 2):
        series = 1.0 - twice * (1.0 / n) * series
    gain_ref[...] = residue_ref[...] * jnp.sqrt(twice * series)
    per_block = jnp.exp(-float(length) * decay)
    carry = jnp.zeros_like(decay)
    for j in range(blocks - 1):
        carry = jnp.where(j < place, per_block * carry + given_ref[j].astype(F32), carry)
    carry_ref[...] = carry
    chunk_id = lax.broadcasted_iota(jnp.int32, (SUB, LANES), 0)
    for h, cols in enumerate(halves(width)):
        rate = [jnp.broadcast_to(decay_ref[m : m + 1, cols], (SUB, LANES)) for m in range(modes)]
        state = []
        for m in range(modes):
            enters = jnp.broadcast_to(carry_ref[m : m + 1, cols], (SUB, LANES))
            run = jnp.where(chunk_id == 0, enters, pltpu.roll(ends_ref[m, :, cols], 1, 0))
            for far in (1, 2, 4):
                moved = jnp.where(chunk_id >= far, pltpu.roll(run, far, 0), 0.0)
                run = run + jnp.exp(-float(steps * far) * rate[m]) * moved
            state.append(run)
        keep = [jnp.exp(-r) for r in rate]
        gain = [jnp.broadcast_to(gain_ref[m : m + 1, cols], (SUB, LANES)) for m in range(modes)]
        skip = jnp.broadcast_to(skip_ref[0:1, cols], (SUB, LANES))
        for p in range(steps):
            signal = signal_ref[p, :, cols]
            state = [keep[m] * state[m] + signal for m in range(modes)]
            terms = [gain[m] * state[m] for m in range(modes)]
            while len(terms) > 1:
                terms = [a + b for a, b in zip(terms[::2], terms[1::2])]
            conv = terms[0].astype(BF16).astype(F32)
            line_ref[h, pl.ds(p, SUB, stride=steps), :] = query_ref[p, :, cols] * (conv + skip * signal)
        gated_ref[:, cols] = line_ref[h].astype(BF16)


def mix_kernel(gated_ref, w_ref, part_ref):
    for y in range(part_ref.shape[0]):
        part_ref[y] = sum(
            jnp.dot(gated_ref[k], w_ref[y, k], preferred_element_type=F32)
            for k in range(gated_ref.shape[0])
        ).astype(BF16)


def sum_kernel(part_ref, out_ref):
    total = part_ref[0].astype(F32)
    for k in range(1, part_ref.shape[0]):
        total = total + part_ref[k].astype(F32)
    out_ref[...] = total.astype(BF16)


def per_device(outer, proj, short_filter, residues, decays, skip, w_out):
    _, width, length = proj.shape
    modes = decays.shape[1]
    features = w_out.shape[1]
    blocks = lax.axis_size("ctx")
    groups = lax.axis_size("ch")
    inner = groups // outer
    steps = length // SUB
    shape = jax.ShapeDtypeStruct

    along_outer = [[a * inner + b for a in range(outer)] for b in range(inner)]
    along_inner = [[a * inner + b for b in range(inner)] for a in range(outer)]
    decays, residues = decays.T, residues.T
    short_filter = short_filter.swapaxes(1, 2)
    w_near = lax.all_to_all(
        w_out.reshape(outer, inner, width, features).swapaxes(0, 1),
        "ch", 0, 0, axis_index_groups=along_inner,
    )
    edge = pl.pallas_call(
        edge_kernel,
        grid=(1,),
        in_specs=[pl.BlockSpec((3, width, LANES), lambda i: (0, 0, length // LANES - 1))],
        out_specs=pl.BlockSpec((SUB, width), lambda i: (0, 0)),
        out_shape=shape((SUB, width), BF16),
    )(proj)
    halo = lax.ppermute(edge, "ctx", [(i, i + 1) for i in range(blocks - 1)])
    signal, query, ends, state = pallas(
        state_kernel,
        (
            shape((steps, SUB, width), F32),
            shape((steps, SUB, width), F32),
            shape((modes, SUB, width), F32),
            shape((blocks, modes, width), BF16),
        ),
        (
            pltpu.VMEM((3, width // LANES, SUB + length, LANES), F32),
            pltpu.VMEM((modes, width), F32),
        ),
    )(proj, halo, short_filter, decays)
    given = lax.all_to_all(state, "ctx", 0, 0)
    place = lax.axis_index("ctx").astype(jnp.int32).reshape(1)
    whole = pl.BlockSpec(memory_space=pltpu.VMEM)
    gated = pallas(
        gate_kernel,
        shape((length, width), BF16),
        (
            pltpu.VMEM((modes, width), F32),
            pltpu.VMEM((modes, width), F32),
            pltpu.VMEM((width // LANES, length, LANES), F32),
        ),
        in_specs=[pl.BlockSpec(memory_space=pltpu.SMEM)] + [whole] * 7,
    )(place, given, signal, query, ends, decays, residues, skip.reshape(1, width))
    near = lax.all_gather(gated, "ch", axis_index_groups=along_outer)
    parts = pallas(mix_kernel, shape((inner, length, features), BF16), in_specs=[whole, whole])(near, w_near)
    parts = lax.all_to_all(parts, "ch", 0, 0, axis_index_groups=along_inner)
    return pallas(sum_kernel, shape((length, features), BF16), in_specs=[whole])(parts)


def solution(mesh):
    groups = mesh.shape["ch"]
    outer = 4 if groups % 4 == 0 else 1
    in_specs = (
        P(None, "ch", "ctx"),
        P(None, "ch", None),
        P("ch", None),
        P("ch", None),
        P("ch"),
        P(None, "ch"),
    )
    return jax.shard_map(
        functools.partial(per_device, outer),
        mesh=mesh,
        in_specs=in_specs,
        out_specs=P("ctx", "ch"),
        check_vma=False,
    )
```

```python
import functools

import jax
import jax.numpy as jnp
from jax import lax
from jax.experimental import pallas as pl
from jax.experimental.pallas import tpu as pltpu
from jax.sharding import PartitionSpec as P

F32 = jnp.float32
BF16 = jnp.bfloat16
LANES = 128
SUB = 8
VMEM_LIMIT = 16 * 1024 * 1024
VMEM_WHOLE = 63 * 1024 * 1024


def pallas(body, out_shape, scratch=(), vmem=VMEM_LIMIT, **kwargs):
    return pl.pallas_call(
        body,
        out_shape=out_shape,
        scratch_shapes=list(scratch),
        compiler_params=pltpu.CompilerParams(vmem_limit_bytes=vmem),
        **kwargs,
    )


def halves(width):
    return [slice(lo, lo + LANES) for lo in range(0, width, LANES)]


def spread(row):
    return jnp.broadcast_to(row, (SUB, LANES))


def fill_line(line_ref, at, block):
    for h, cols in enumerate(halves(block.shape[1])):
        line_ref[at, h, :SUB, :] = jnp.zeros((SUB, LANES), F32)
        line_ref[at, h, SUB:, :] = block[:, cols]


def short_mix(line_ref, at, h, tap, steps):
    def rows(step):
        return line_ref[at, h, pl.ds(SUB + step, SUB, stride=steps), :]

    back2, back1 = rows(-2), rows(-1)
    for p in range(steps):
        here = rows(p)
        yield tap[0] * here + tap[1] * back1 + tap[2] * back2
        back2, back1 = back1, here


def signal_steps(k_line, v_line, filter_ref, h, cols, steps):
    chunk_id = lax.broadcasted_iota(jnp.int32, (SUB, LANES), 0)
    mixes = [
        short_mix(line_ref, at, h, [spread(filter_ref[i, m : m + 1, cols]) for m in range(3)], steps)
        for i, (line_ref, at) in enumerate((k_line, v_line), start=1)
    ]
    for p, (k, v) in enumerate(zip(*mixes)):
        signal = (k * v).astype(BF16).astype(F32)
        yield jnp.where(chunk_id == 0, 0.0, signal) if p < 2 else signal


def state_kernel(k_ref, v_ref, q_edge_ref, filter_ref, decay_ref, sent_ref, line_ref, sums_ref):
    width, length = k_ref.shape[1:]
    steps = length // SUB
    modes = decay_ref.shape[0]
    blocks = [ref[0].astype(F32).T for ref in (k_ref, v_ref)]
    for i, block in enumerate(blocks):
        fill_line(line_ref, i, block)
    chunk_id = lax.broadcasted_iota(jnp.int32, (SUB, LANES), 0)
    from_end = float(steps) * (SUB - 1 - chunk_id).astype(F32)
    for h, cols in enumerate(halves(width)):
        rate = [spread(decay_ref[m : m + 1, cols]) for m in range(modes)]
        keep = [jnp.exp(-r) for r in rate]
        state = [jnp.zeros((SUB, LANES), F32) for _ in range(modes)]
        for signal in signal_steps((line_ref, 0), (line_ref, 1), filter_ref, h, cols, steps):
            state = [keep[m] * state[m] + signal for m in range(modes)]
        for m in range(modes):
            weight = jnp.exp(-rate[m] * from_end)
            sums_ref[h * modes + m : h * modes + m + 1, :] = jnp.sum(weight * state[m], axis=0, keepdims=True)
    last_q = q_edge_ref[0].astype(F32).T[-2:, :]
    edges = [blocks[0][-2:], blocks[1][-2:], blocks[0][:2], blocks[1][:2]]
    at = 2 * modes
    for h, cols in enumerate(halves(width)):
        for e, edge in enumerate(edges):
            sums_ref[at + h * SUB + 2 * e : at + h * SUB + 2 * e + 2, :] = edge[:, cols]
        sums_ref[at + 2 * SUB + 2 * h : at + 2 * SUB + 2 * h + 2, :] = last_q[:, cols]
    sums_ref[at + 2 * SUB + 4 :, :] = jnp.zeros((4, LANES), F32)
    sent = sums_ref[...].astype(BF16)
    for j in range(sent_ref.shape[0]):
        sent_ref[j] = sent


def prepare_kernel(proj_ref, filter_ref, decay_ref, signal_ref, query_ref, first_ref, ends_ref, line_ref):
    _, width, length = proj_ref.shape
    steps = length // SUB
    modes = decay_ref.shape[0]
    for i in range(3):
        fill_line(line_ref, i, proj_ref[i].astype(F32).T)
    for h, cols in enumerate(halves(width)):
        tap = [spread(filter_ref[0, m : m + 1, cols]) for m in range(3)]
        mixes = list(short_mix(line_ref, 0, h, tap, steps))
        first_ref[0, :, cols], first_ref[1, :, cols] = mixes[:2]
        for p in range(0, steps, 2):
            query_ref[p // 2, :, cols] = jnp.concatenate(mixes[p : p + 2], axis=0).astype(BF16)
        keep = [jnp.exp(-spread(decay_ref[m : m + 1, cols])) for m in range(modes)]
        state = [jnp.zeros((SUB, LANES), F32) for _ in range(modes)]
        pair = []
        for p, signal in enumerate(signal_steps((line_ref, 1), (line_ref, 2), filter_ref, h, cols, steps)):
            pair.append(signal)
            if p % 2:
                signal_ref[p // 2, :, cols] = jnp.concatenate(pair, axis=0).astype(BF16)
                pair = []
            state = [keep[m] * state[m] + signal for m in range(modes)]
        for m in range(modes):
            ends_ref[m, :, cols] = state[m]


def first_signals(taps_k, taps_v, edge, last):
    def mixed(tap, first, before):
        zero = tap[0] * first[0:1] + tap[1] * before[1:2] + tap[2] * before[0:1]
        one = tap[0] * first[1:2] + tap[1] * first[0:1] + tap[2] * before[1:2]
        return zero, one

    k = mixed(taps_k, edge[4:6], last[0:2])
    v = mixed(taps_v, edge[6:8], last[2:4])
    return [(a * b).astype(BF16).astype(F32) for a, b in zip(k, v)]


def gate_kernel(
    place_ref, given_ref, signal_ref, query_ref, first_ref, ends_ref, filter_ref, decay_ref, residue_ref, skip_ref,
    gated_ref,
    line_ref,
):
    blocks = given_ref.shape[0]
    modes, width = decay_ref.shape
    steps = 2 * signal_ref.shape[0]
    length = steps * SUB
    at = 2 * modes
    place = place_ref[0]
    chunk_id = lax.broadcasted_iota(jnp.int32, (SUB, LANES), 0)
    own = given_ref[place].astype(F32)
    before = given_ref[jnp.maximum(place - 1, 0)].astype(F32)
    before = jnp.where(place > 0, before, 0.0)
    for h, cols in enumerate(halves(width)):
        decay = decay_ref[:, cols]
        twice = 2.0 * decay
        series = jnp.ones_like(twice)
        for n in (8, 7, 6, 5, 4, 3, 2):
            series = 1.0 - twice * (1.0 / n) * series
        weight = residue_ref[:, cols] * jnp.sqrt(twice * series)
        taps = [[filter_ref[i, m : m + 1, cols] for m in range(3)] for i in range(3)]
        per_block = jnp.exp(-float(length) * decay)
        age0 = jnp.exp(-float(length - 1) * decay)
        age1 = jnp.exp(-float(length - 2) * decay)
        carry = jnp.zeros_like(decay)
        last = jnp.zeros((SUB, LANES), F32)
        for j in range(blocks - 1):
            there = given_ref[j].astype(F32)
            edge = there[at + h * SUB : at + (h + 1) * SUB]
            zero, one = first_signals(taps[1], taps[2], edge, last)
            gone = there[h * modes : (h + 1) * modes] + age0 * zero + age1 * one
            carry = jnp.where(j < place, per_block * carry + gone, carry)
            last = edge
        rows = slice(at + h * SUB, at + (h + 1) * SUB)
        firsts = first_signals(taps[1], taps[2], own[rows], before[rows])
        q_last = before[at + 2 * SUB + 2 * h : at + 2 * SUB + 2 * h + 2]
        q_more = [taps[0][1] * q_last[1:2] + taps[0][2] * q_last[0:1], taps[0][2] * q_last[1:2]]
        rate = [spread(decay[m : m + 1]) for m in range(modes)]
        keep = [jnp.exp(-r) for r in rate]
        state = []
        for m in range(modes):
            end = ends_ref[m, :, cols]
            more = jnp.exp(-float(steps - 1) * decay[m : m + 1]) * firsts[0]
            more = more + jnp.exp(-float(steps - 2) * decay[m : m + 1]) * firsts[1]
            end = jnp.where(chunk_id == 0, end + spread(more), end)
            run = jnp.where(chunk_id == 0, spread(carry[m : m + 1]), pltpu.roll(end, 1, 0))
            for far in (1, 2, 4):
                moved = jnp.where(chunk_id >= far, pltpu.roll(run, far, 0), 0.0)
                run = run + jnp.exp(-float(steps * far) * rate[m]) * moved
            state.append(run)
        gain = [spread(weight[m : m + 1]) for m in range(modes)]
        skip = spread(skip_ref[0:1, cols])
        for p in range(steps):
            if p % 2 == 0:
                signals = signal_ref[p // 2, :, cols].astype(F32)
                queries = query_ref[p // 2, :, cols].astype(F32)
            signal = signals[p % 2 * SUB : (p % 2 + 1) * SUB]
            query = queries[p % 2 * SUB : (p % 2 + 1) * SUB]
            if p < 2:
                signal = jnp.where(chunk_id == 0, spread(firsts[p]), signal)
                full = (first_ref[p, :, cols] + spread(q_more[p])).astype(BF16).astype(F32)
                query = jnp.where(chunk_id == 0, full, query)
            state = [keep[m] * state[m] + signal for m in range(modes)]
            terms = [gain[m] * state[m] for m in range(modes)]
            while len(terms) > 1:
                terms = [a + b for a, b in zip(terms[::2], terms[1::2])]
            conv = terms[0].astype(BF16).astype(F32)
            line_ref[h, pl.ds(p, SUB, stride=steps), :] = query * (conv + skip * signal)
        gated_ref[:, cols] = line_ref[h].astype(BF16)


def roll_kernel(place_ref, w_ref, *refs):
    outs, sems = refs[:-1], refs[-1]
    inner = w_ref.shape[1]
    copies = [
        pltpu.make_async_copy(w_ref.at[:, lax.rem(place_ref[0] + k, inner)], out, sems.at[k])
        for k, out in enumerate(outs)
    ]
    for copy in copies:
        copy.start()
    for copy in copies:
        copy.wait()


def mix_kernel(place_ref, gated_ref, own_ref, *refs):
    w_refs, part_ref = (own_ref,) + refs[:-1], refs[-1]
    inner = part_ref.shape[0]
    for k, w_ref in enumerate(w_refs):
        part_ref[lax.rem(place_ref[0] - k + inner, inner)] = sum(
            jnp.dot(gated_ref[z], w_ref[z], preferred_element_type=F32)
            for z in range(gated_ref.shape[0])
        ).astype(BF16)


def sum_kernel(part_ref, out_ref):
    total = part_ref[0].astype(F32)
    for k in range(1, part_ref.shape[0]):
        total = total + part_ref[k].astype(F32)
    out_ref[...] = total.astype(BF16)


def per_device(outer, proj, short_filter, residues, decays, skip, w_out):
    _, width, length = proj.shape
    modes = decays.shape[1]
    features = w_out.shape[1]
    blocks = lax.axis_size("ctx")
    groups = lax.axis_size("ch")
    inner = groups // outer
    steps = length // SUB
    shape = jax.ShapeDtypeStruct

    along_outer = [[a * inner + b for a in range(outer)] for b in range(inner)]
    along_inner = [[a * inner + b for b in range(inner)] for a in range(outer)]
    decays, residues = decays.T, residues.T
    short_filter = short_filter.swapaxes(1, 2)
    place = lax.axis_index("ctx").astype(jnp.int32).reshape(1)
    place_y = lax.rem(lax.axis_index("ch"), inner).astype(jnp.int32).reshape(1)
    whole = pl.BlockSpec(memory_space=pltpu.VMEM)
    scalar = pl.BlockSpec(memory_space=pltpu.SMEM)
    far = pl.BlockSpec(memory_space=pl.ANY)

    def full(*dims):
        return pl.BlockSpec(dims, lambda i: (0,) * len(dims))

    def one(i, lanes, at):
        return pl.BlockSpec((1, width, lanes), lambda g: (i, 0, at))

    sent_rows = 2 * modes + 3 * SUB
    sent = pallas(
        state_kernel,
        shape((blocks, sent_rows, LANES), BF16),
        (
            pltpu.VMEM((2, width // LANES, SUB + length, LANES), F32),
            pltpu.VMEM((sent_rows, LANES), F32),
        ),
        vmem=VMEM_WHOLE,
        grid=(1,),
        in_specs=[
            one(1, length, 0),
            one(2, length, 0),
            one(0, LANES, length // LANES - 1),
            full(3, 3, width),
            full(modes, width),
        ],
        out_specs=full(blocks, sent_rows, LANES),
    )(proj, proj, proj, short_filter, decays)
    given = lax.all_to_all(sent, "ctx", 0, 0)
    proj, sent = lax.optimization_barrier((proj, sent))
    signal, query, first, ends = pallas(
        prepare_kernel,
        (
            shape((steps // 2, 2 * SUB, width), BF16),
            shape((steps // 2, 2 * SUB, width), BF16),
            shape((2, SUB, width), F32),
            shape((modes, SUB, width), F32),
        ),
        (pltpu.VMEM((3, width // LANES, SUB + length, LANES), F32),),
        in_specs=[whole] * 3,
        cost_estimate=pl.CostEstimate(flops=4000000, bytes_accessed=1000000, transcendentals=0),
    )(proj, short_filter, decays)
    w_parts = w_out.reshape(outer, inner, width, features)
    place_y, first = lax.optimization_barrier((place_y, first))
    rolled = pallas(
        roll_kernel,
        [shape((outer, width, features), BF16)] * inner,
        (pltpu.SemaphoreType.DMA((inner,)),),
        in_specs=[scalar, whole],
        out_specs=[whole] + [far] * (inner - 1),
    )(place_y, w_parts)
    w_near = [
        lax.ppermute(
            part, "ch",
            [(a * inner + b, a * inner + (b + k + 1) % inner) for a in range(outer) for b in range(inner)],
        )
        for k, part in enumerate(rolled[1:])
    ]
    gated = pallas(
        gate_kernel,
        shape((length, width), BF16),
        (pltpu.VMEM((width // LANES, length, LANES), F32),),
        in_specs=[scalar] + [whole] * 9,
    )(place, given, signal, query, first, ends, short_filter, decays, residues, skip.reshape(1, width))
    near = lax.all_gather(gated, "ch", axis_index_groups=along_outer)
    parts = pallas(
        mix_kernel,
        shape((inner, length, features), BF16),
        in_specs=[scalar] + [whole] * (1 + inner),
    )(place_y, near, rolled[0], *w_near)
    parts = lax.all_to_all(parts, "ch", 0, 0, axis_index_groups=along_inner)
    return pallas(sum_kernel, shape((length, features), BF16), in_specs=[whole])(parts)


def solution(mesh):
    groups = mesh.shape["ch"]
    outer = 4 if groups % 4 == 0 else 1
    in_specs = (
        P(None, "ch", "ctx"),
        P(None, "ch", None),
        P("ch", None),
        P("ch", None),
        P("ch"),
        P(None, "ch"),
    )
    return jax.shard_map(
        functools.partial(per_device, outer),
        mesh=mesh,
        in_specs=in_specs,
        out_specs=P("ctx", "ch"),
        check_vma=False,
    )
```

```python
import functools

import jax
import jax.numpy as jnp
from jax import lax
from jax.experimental import pallas as pl
from jax.experimental.pallas import tpu as pltpu
from jax.sharding import PartitionSpec as P

F32 = jnp.float32
BF16 = jnp.bfloat16
LANES = 128
SUB = 8
VMEM_LIMIT = 16 * 1024 * 1024
VMEM_MOST = 16 * 1024 * 1024
VMEM_WHOLE = 63 * 1024 * 1024


def pallas(body, out_shape, scratch=(), vmem=VMEM_LIMIT, **kwargs):
    return pl.pallas_call(
        body,
        out_shape=out_shape,
        scratch_shapes=list(scratch),
        compiler_params=pltpu.CompilerParams(vmem_limit_bytes=vmem),
        **kwargs,
    )


def halves(width):
    return [slice(lo, lo + LANES) for lo in range(0, width, LANES)]


def spread(row):
    return jnp.broadcast_to(row, (SUB, LANES))


def fill_line(line_ref, at, block):
    for h, cols in enumerate(halves(block.shape[1])):
        line_ref[at, h, :SUB, :] = jnp.zeros((SUB, LANES), F32)
        line_ref[at, h, SUB:, :] = block[:, cols]


def short_mix(line_ref, at, h, tap, steps):
    def rows(step):
        return line_ref[at, h, pl.ds(SUB + step, SUB, stride=steps), :]

    back2, back1 = rows(-2), rows(-1)
    for p in range(steps):
        here = rows(p)
        yield tap[0] * here + tap[1] * back1 + tap[2] * back2
        back2, back1 = back1, here


def w_copies(place, w_ref, outs, held_ref, come, go, ahead):
    inner = w_ref.shape[1]
    loads = [
        pltpu.make_async_copy(w_ref.at[:, lax.rem(place + k, inner)], held_ref.at[n], come.at[n])
        for n, k in enumerate(ahead)
    ]
    stores = [pltpu.make_async_copy(held_ref.at[n], out, go.at[n]) for n, out in enumerate(outs)]
    return loads, stores


def signal_steps(k_line, v_line, filter_ref, h, cols, steps):
    chunk_id = lax.broadcasted_iota(jnp.int32, (SUB, LANES), 0)
    mixes = [
        short_mix(line_ref, at, h, [spread(filter_ref[i, m : m + 1, cols]) for m in range(3)], steps)
        for i, (line_ref, at) in enumerate((k_line, v_line), start=1)
    ]
    for p, (k, v) in enumerate(zip(*mixes)):
        signal = (k * v).astype(BF16).astype(F32)
        yield jnp.where(chunk_id == 0, 0.0, signal) if p < 2 else signal


def state_kernel(ahead, place_ref, proj_hbm, filter_hbm, decay_hbm, w_hbm, sent_ref, *refs):
    w_outs, refs = refs[: len(ahead)], refs[len(ahead) :]
    kv_ref, q_edge_ref, filter_ref, decay_ref, line_ref, sums_ref, held_ref, sems, come, go = refs
    _, width, length = kv_ref.shape
    steps = length // SUB
    modes = decay_ref.shape[0]
    ends = pl.ds(length - LANES, LANES)
    pairs = [
        (proj_hbm.at[1], kv_ref.at[0]),
        (proj_hbm.at[2], kv_ref.at[1]),
        (filter_hbm, filter_ref),
        (decay_hbm, decay_ref),
        (proj_hbm.at[0, :, ends], q_edge_ref),
    ]
    loads = [pltpu.make_async_copy(a, b, sems.at[n]) for n, (a, b) in enumerate(pairs)]
    w_loads, w_stores = w_copies(place_ref[0], w_hbm, w_outs, held_ref, come, go, ahead)
    for load in loads + w_loads:
        load.start()
    blocks = []
    for i in range(2):
        loads[i].wait()
        blocks.append(kv_ref[i].astype(F32).T)
        fill_line(line_ref, i, blocks[i])
    for load in loads[2:]:
        load.wait()
    chunk_id = lax.broadcasted_iota(jnp.int32, (SUB, LANES), 0)
    from_end = float(steps) * (SUB - 1 - chunk_id).astype(F32)
    for h, cols in enumerate(halves(width)):
        rate = [spread(decay_ref[m : m + 1, cols]) for m in range(modes)]
        keep = [jnp.exp(-r) for r in rate]
        state = [jnp.zeros((SUB, LANES), F32) for _ in range(modes)]
        for signal in signal_steps((line_ref, 0), (line_ref, 1), filter_ref, h, cols, steps):
            state = [keep[m] * state[m] + signal for m in range(modes)]
        for m in range(modes):
            weight = jnp.exp(-rate[m] * from_end)
            sums_ref[h * modes + m : h * modes + m + 1, :] = jnp.sum(weight * state[m], axis=0, keepdims=True)
        if h == 0:
            for load, store in zip(w_loads, w_stores):
                load.wait()
                store.start()
    last_q = q_edge_ref[...].astype(F32).T[-2:, :]
    edges = [blocks[0][-2:], blocks[1][-2:], blocks[0][:2], blocks[1][:2]]
    at = 2 * modes
    for h, cols in enumerate(halves(width)):
        for e, edge in enumerate(edges):
            sums_ref[at + h * SUB + 2 * e : at + h * SUB + 2 * e + 2, :] = edge[:, cols]
        sums_ref[at + 2 * SUB + 2 * h : at + 2 * SUB + 2 * h + 2, :] = last_q[:, cols]
    sums_ref[at + 2 * SUB + 4 :, :] = jnp.zeros((4, LANES), F32)
    sent = sums_ref[...].astype(BF16)
    for j in range(sent_ref.shape[0]):
        sent_ref[j] = sent
    for store in w_stores:
        store.wait()


def prepare_kernel(
    ahead, place_ref, proj_ref, filter_ref, decay_ref, w_hbm, signal_ref, query_ref, first_ref, ends_ref, *refs
):
    w_outs, (line_ref, held_ref, come, go) = refs[: len(ahead)], refs[len(ahead) :]
    w_loads, w_stores = w_copies(place_ref[0], w_hbm, w_outs, held_ref, come, go, ahead)
    for load in w_loads:
        load.start()
    _, width, length = proj_ref.shape
    steps = length // SUB
    modes = decay_ref.shape[0]
    for i in range(3):
        fill_line(line_ref, i, proj_ref[i].astype(F32).T)
    for h, cols in enumerate(halves(width)):
        tap = [spread(filter_ref[0, m : m + 1, cols]) for m in range(3)]
        mixes = list(short_mix(line_ref, 0, h, tap, steps))
        first_ref[0, :, cols], first_ref[1, :, cols] = mixes[:2]
        for p in range(0, steps, 2):
            query_ref[p // 2, :, cols] = jnp.concatenate(mixes[p : p + 2], axis=0).astype(BF16)
        keep = [jnp.exp(-spread(decay_ref[m : m + 1, cols])) for m in range(modes)]
        state = [jnp.zeros((SUB, LANES), F32) for _ in range(modes)]
        pair = []
        for p, signal in enumerate(signal_steps((line_ref, 1), (line_ref, 2), filter_ref, h, cols, steps)):
            pair.append(signal)
            if p % 2:
                signal_ref[p // 2, :, cols] = jnp.concatenate(pair, axis=0).astype(BF16)
                pair = []
            state = [keep[m] * state[m] + signal for m in range(modes)]
        for m in range(modes):
            ends_ref[m, :, cols] = state[m]
        if h == 0:
            for load, store in zip(w_loads, w_stores):
                load.wait()
                store.start()
    for store in w_stores:
        store.wait()


def first_signals(taps_k, taps_v, edge, last):
    def mixed(tap, first, before):
        zero = tap[0] * first[0:1] + tap[1] * before[1:2] + tap[2] * before[0:1]
        one = tap[0] * first[1:2] + tap[1] * first[0:1] + tap[2] * before[1:2]
        return zero, one

    k = mixed(taps_k, edge[4:6], last[0:2])
    v = mixed(taps_v, edge[6:8], last[2:4])
    return [(a * b).astype(BF16).astype(F32) for a, b in zip(k, v)]


def gate_kernel(
    place_ref, given_ref, signal_ref, query_ref, first_ref, ends_ref, filter_ref, decay_ref, residue_ref, skip_ref,
    gated_ref,
    line_ref,
):
    blocks = given_ref.shape[0]
    modes, width = decay_ref.shape
    steps = 2 * signal_ref.shape[0]
    length = steps * SUB
    at = 2 * modes
    place = place_ref[0]
    chunk_id = lax.broadcasted_iota(jnp.int32, (SUB, LANES), 0)
    own = given_ref[place].astype(F32)
    before = given_ref[jnp.maximum(place - 1, 0)].astype(F32)
    before = jnp.where(place > 0, before, 0.0)
    for h, cols in enumerate(halves(width)):
        decay = decay_ref[:, cols]
        twice = 2.0 * decay
        series = jnp.ones_like(twice)
        for n in (8, 7, 6, 5, 4, 3, 2):
            series = 1.0 - twice * (1.0 / n) * series
        weight = residue_ref[:, cols] * jnp.sqrt(twice * series)
        taps = [[filter_ref[i, m : m + 1, cols] for m in range(3)] for i in range(3)]
        per_block = jnp.exp(-float(length) * decay)
        age0 = jnp.exp(-float(length - 1) * decay)
        age1 = jnp.exp(-float(length - 2) * decay)
        carry = jnp.zeros_like(decay)
        last = jnp.zeros((SUB, LANES), F32)
        for j in range(blocks - 1):
            there = given_ref[j].astype(F32)
            edge = there[at + h * SUB : at + (h + 1) * SUB]
            zero, one = first_signals(taps[1], taps[2], edge, last)
            gone = there[h * modes : (h + 1) * modes] + age0 * zero + age1 * one
            carry = jnp.where(j < place, per_block * carry + gone, carry)
            last = edge
        rows = slice(at + h * SUB, at + (h + 1) * SUB)
        firsts = first_signals(taps[1], taps[2], own[rows], before[rows])
        q_last = before[at + 2 * SUB + 2 * h : at + 2 * SUB + 2 * h + 2]
        q_more = [taps[0][1] * q_last[1:2] + taps[0][2] * q_last[0:1], taps[0][2] * q_last[1:2]]
        rate = [spread(decay[m : m + 1]) for m in range(modes)]
        keep = [jnp.exp(-r) for r in rate]
        state = []
        for m in range(modes):
            end = ends_ref[m, :, cols]
            more = jnp.exp(-float(steps - 1) * decay[m : m + 1]) * firsts[0]
            more = more + jnp.exp(-float(steps - 2) * decay[m : m + 1]) * firsts[1]
            end = jnp.where(chunk_id == 0, end + spread(more), end)
            run = jnp.where(chunk_id == 0, spread(carry[m : m + 1]), pltpu.roll(end, 1, 0))
            for far in (1, 2, 4):
                moved = jnp.where(chunk_id >= far, pltpu.roll(run, far, 0), 0.0)
                run = run + jnp.exp(-float(steps * far) * rate[m]) * moved
            state.append(run)
        gain = [spread(weight[m : m + 1]) for m in range(modes)]
        skip = spread(skip_ref[0:1, cols])
        for p in range(steps):
            if p % 2 == 0:
                signals = signal_ref[p // 2, :, cols].astype(F32)
                queries = query_ref[p // 2, :, cols].astype(F32)
            signal = signals[p % 2 * SUB : (p % 2 + 1) * SUB]
            query = queries[p % 2 * SUB : (p % 2 + 1) * SUB]
            if p < 2:
                signal = jnp.where(chunk_id == 0, spread(firsts[p]), signal)
                full = (first_ref[p, :, cols] + spread(q_more[p])).astype(BF16).astype(F32)
                query = jnp.where(chunk_id == 0, full, query)
            state = [keep[m] * state[m] + signal for m in range(modes)]
            terms = [gain[m] * state[m] for m in range(modes)]
            while len(terms) > 1:
                terms = [a + b for a, b in zip(terms[::2], terms[1::2])]
            conv = terms[0].astype(BF16).astype(F32)
            line_ref[h, pl.ds(p, SUB, stride=steps), :] = query * (conv + skip * signal)
        gated_ref[:, cols] = line_ref[h].astype(BF16)


def mix_kernel(place_ref, gated_ref, own_ref, *refs):
    w_refs, part_ref = (own_ref,) + refs[:-1], refs[-1]
    inner = part_ref.shape[0]
    for k, w_ref in enumerate(w_refs):
        part_ref[lax.rem(place_ref[0] - k + inner, inner)] = sum(
            jnp.dot(gated_ref[z], w_ref[z], preferred_element_type=F32)
            for z in range(gated_ref.shape[0])
        ).astype(BF16)


def sum_kernel(part_ref, out_ref):
    total = part_ref[0].astype(F32)
    for k in range(1, part_ref.shape[0]):
        total = total + part_ref[k].astype(F32)
    out_ref[...] = total.astype(BF16)


def per_device(outer, proj, short_filter, residues, decays, skip, w_out):
    _, width, length = proj.shape
    modes = decays.shape[1]
    features = w_out.shape[1]
    blocks = lax.axis_size("ctx")
    groups = lax.axis_size("ch")
    inner = groups // outer
    steps = length // SUB
    shape = jax.ShapeDtypeStruct

    along_outer = [[a * inner + b for a in range(outer)] for b in range(inner)]
    along_inner = [[a * inner + b for b in range(inner)] for a in range(outer)]
    decays, residues = decays.T, residues.T
    short_filter = short_filter.swapaxes(1, 2)
    place = lax.axis_index("ctx").astype(jnp.int32).reshape(1)
    place_y = lax.rem(lax.axis_index("ch"), inner).astype(jnp.int32).reshape(1)
    whole = pl.BlockSpec(memory_space=pltpu.VMEM)
    scalar = pl.BlockSpec(memory_space=pltpu.SMEM)
    far = pl.BlockSpec(memory_space=pl.ANY)

    sent_rows = 2 * modes + 3 * SUB
    w_parts = w_out.reshape(outer, inner, width, features)
    w_block = shape((outer, width, features), BF16)
    soon, later = (1,), (0, 2, 3)
    sent, *w_soon = pallas(
        functools.partial(state_kernel, soon),
        [shape((blocks, sent_rows, LANES), BF16)] + [w_block] * len(soon),
        (
            pltpu.VMEM((2, width, length), BF16),
            pltpu.VMEM((width, LANES), BF16),
            pltpu.VMEM((3, 3, width), F32),
            pltpu.VMEM((modes, width), F32),
            pltpu.VMEM((2, width // LANES, SUB + length, LANES), F32),
            pltpu.VMEM((sent_rows, LANES), F32),
            pltpu.VMEM((len(soon), outer, width, features), BF16),
            pltpu.SemaphoreType.DMA((5,)),
            pltpu.SemaphoreType.DMA((len(soon),)),
            pltpu.SemaphoreType.DMA((len(soon),)),
        ),
        vmem=VMEM_WHOLE,
        in_specs=[scalar] + [far] * 4,
        out_specs=[whole] + [far] * len(soon),
    )(place_y, proj, short_filter, decays, w_parts)
    given = lax.all_to_all(sent, "ctx", 0, 0)
    proj, place_later, sent = lax.optimization_barrier((proj, place_y, sent))
    signal, query, first, ends, *w_later = pallas(
        functools.partial(prepare_kernel, later),
        [
            shape((steps // 2, 2 * SUB, width), BF16),
            shape((steps // 2, 2 * SUB, width), BF16),
            shape((2, SUB, width), F32),
            shape((modes, SUB, width), F32),
        ]
        + [w_block] * len(later),
        (
            pltpu.VMEM((3, width // LANES, SUB + length, LANES), F32),
            pltpu.VMEM((len(later), outer, width, features), BF16),
            pltpu.SemaphoreType.DMA((len(later),)),
            pltpu.SemaphoreType.DMA((len(later),)),
        ),
        vmem=VMEM_MOST,
        in_specs=[scalar] + [whole] * 3 + [far],
        out_specs=[whole] * 4 + [far] * len(later),
        cost_estimate=pl.CostEstimate(flops=4000000, bytes_accessed=4000000, transcendentals=0),
    )(place_later, proj, short_filter, decays, w_parts)
    rolled = dict(zip(soon + later, w_soon + w_later))
    w_near = [
        lax.ppermute(
            rolled[k], "ch",
            [(a * inner + b, a * inner + (b + k) % inner) for a in range(outer) for b in range(inner)],
        )
        for k in range(1, inner)
    ]
    gated = pallas(
        gate_kernel,
        shape((length, width), BF16),
        (pltpu.VMEM((width // LANES, length, LANES), F32),),
        in_specs=[scalar] + [whole] * 9,
    )(place, given, signal, query, first, ends, short_filter, decays, residues, skip.reshape(1, width))
    near = lax.all_gather(gated, "ch", axis_index_groups=along_outer)
    parts = pallas(
        mix_kernel,
        shape((inner, length, features), BF16),
        in_specs=[scalar] + [whole] * (1 + inner),
    )(place_y, near, rolled[0], *w_near)
    parts = lax.all_to_all(parts, "ch", 0, 0, axis_index_groups=along_inner)
    return pallas(sum_kernel, shape((length, features), BF16), in_specs=[whole])(parts)


def solution(mesh):
    groups = mesh.shape["ch"]
    outer = 4 if groups % 4 == 0 else 1
    in_specs = (
        P(None, "ch", "ctx"),
        P(None, "ch", None),
        P("ch", None),
        P("ch", None),
        P("ch"),
        P(None, "ch"),
    )
    return jax.shard_map(
        functools.partial(per_device, outer),
        mesh=mesh,
        in_specs=in_specs,
        out_specs=P("ctx", "ch"),
        check_vma=False,
    )
```

```python
import functools

import jax
import jax.numpy as jnp
from jax import lax
from jax.experimental import pallas as pl
from jax.experimental.pallas import tpu as pltpu
from jax.sharding import PartitionSpec as P

F32 = jnp.float32
BF16 = jnp.bfloat16
LANES = 128
SUB = 8
VMEM_LIMIT = 16 * 1024 * 1024
VMEM_WHOLE = 63 * 1024 * 1024


def pallas(body, out_shape, scratch=(), vmem=VMEM_LIMIT, **kwargs):
    return pl.pallas_call(
        body,
        out_shape=out_shape,
        scratch_shapes=list(scratch),
        compiler_params=pltpu.CompilerParams(vmem_limit_bytes=vmem),
        **kwargs,
    )


def halves(width):
    return [slice(lo, lo + LANES) for lo in range(0, width, LANES)]


def spread(row):
    return jnp.broadcast_to(row, (SUB, LANES))


def fill_line(line_ref, at, block):
    for h, cols in enumerate(halves(block.shape[1])):
        line_ref[at, h, :SUB, :] = jnp.zeros((SUB, LANES), F32)
        line_ref[at, h, SUB:, :] = block[:, cols]


def short_mix(line_ref, at, h, tap, steps):
    def rows(step):
        return line_ref[at, h, pl.ds(SUB + step, SUB, stride=steps), :]

    back2, back1 = rows(-2), rows(-1)
    for p in range(steps):
        here = rows(p)
        yield tap[0] * here + tap[1] * back1 + tap[2] * back2
        back2, back1 = back1, here


def signal_steps(k_line, v_line, filter_ref, h, cols, steps):
    chunk_id = lax.broadcasted_iota(jnp.int32, (SUB, LANES), 0)
    mixes = [
        short_mix(line_ref, at, h, [spread(filter_ref[i, m : m + 1, cols]) for m in range(3)], steps)
        for i, (line_ref, at) in enumerate((k_line, v_line), start=1)
    ]
    for p, (k, v) in enumerate(zip(*mixes)):
        signal = (k * v).astype(BF16).astype(F32)
        yield jnp.where(chunk_id == 0, 0.0, signal) if p < 2 else signal


def state_kernel(
    q_ref, k_ref, v_ref, filter_ref, decay_ref,
    sent_ref, signal_ref, query_ref, first_ref, ends_ref,
    line_ref, sums_ref,
):
    width, length = k_ref.shape[1:]
    steps = length // SUB
    modes = decay_ref.shape[0]
    blocks = [ref[0].astype(F32).T for ref in (q_ref, k_ref, v_ref)]
    for i, block in enumerate(blocks):
        fill_line(line_ref, i, block)
    chunk_id = lax.broadcasted_iota(jnp.int32, (SUB, LANES), 0)
    from_end = float(steps) * (SUB - 1 - chunk_id).astype(F32)
    for h, cols in enumerate(halves(width)):
        rate = [spread(decay_ref[m : m + 1, cols]) for m in range(modes)]
        keep = [jnp.exp(-r) for r in rate]
        state = [jnp.zeros((SUB, LANES), F32) for _ in range(modes)]
        pair = []
        for p, signal in enumerate(signal_steps((line_ref, 1), (line_ref, 2), filter_ref, h, cols, steps)):
            pair.append(signal)
            if p % 2:
                signal_ref[p // 2, :, cols] = jnp.concatenate(pair, axis=0).astype(BF16)
                pair = []
            state = [keep[m] * state[m] + signal for m in range(modes)]
        for m in range(modes):
            ends_ref[m, :, cols] = state[m]
            weight = jnp.exp(-rate[m] * from_end)
            sums_ref[h * modes + m : h * modes + m + 1, :] = jnp.sum(weight * state[m], axis=0, keepdims=True)
        tap = [spread(filter_ref[0, m : m + 1, cols]) for m in range(3)]
        mixes = list(short_mix(line_ref, 0, h, tap, steps))
        first_ref[0, :, cols], first_ref[1, :, cols] = mixes[:2]
        for p in range(0, steps, 2):
            query_ref[p // 2, :, cols] = jnp.concatenate(mixes[p : p + 2], axis=0).astype(BF16)
    edges = [blocks[1][-2:], blocks[2][-2:], blocks[1][:2], blocks[2][:2]]
    at = 2 * modes
    for h, cols in enumerate(halves(width)):
        for e, edge in enumerate(edges):
            sums_ref[at + h * SUB + 2 * e : at + h * SUB + 2 * e + 2, :] = edge[:, cols]
        sums_ref[at + 2 * SUB + 2 * h : at + 2 * SUB + 2 * h + 2, :] = blocks[0][-2:, cols]
    sums_ref[at + 2 * SUB + 4 :, :] = jnp.zeros((4, LANES), F32)
    sent = sums_ref[...].astype(BF16)
    for j in range(sent_ref.shape[0]):
        sent_ref[j] = sent


def first_signals(taps_k, taps_v, edge, last):
    def mixed(tap, first, before):
        zero = tap[0] * first[0:1] + tap[1] * before[1:2] + tap[2] * before[0:1]
        one = tap[0] * first[1:2] + tap[1] * first[0:1] + tap[2] * before[1:2]
        return zero, one

    k = mixed(taps_k, edge[4:6], last[0:2])
    v = mixed(taps_v, edge[6:8], last[2:4])
    return [(a * b).astype(BF16).astype(F32) for a, b in zip(k, v)]


def gate_kernel(
    place_ref, given_ref, signal_ref, query_ref, first_ref, ends_ref, filter_ref, decay_ref, residue_ref, skip_ref,
    gated_ref,
    line_ref,
):
    blocks = given_ref.shape[0]
    modes, width = decay_ref.shape
    steps = 2 * signal_ref.shape[0]
    length = steps * SUB
    at = 2 * modes
    place = place_ref[0]
    chunk_id = lax.broadcasted_iota(jnp.int32, (SUB, LANES), 0)
    own = given_ref[place].astype(F32)
    before = given_ref[jnp.maximum(place - 1, 0)].astype(F32)
    before = jnp.where(place > 0, before, 0.0)
    for h, cols in enumerate(halves(width)):
        decay = decay_ref[:, cols]
        twice = 2.0 * decay
        series = jnp.ones_like(twice)
        for n in (8, 7, 6, 5, 4, 3, 2):
            series = 1.0 - twice * (1.0 / n) * series
        weight = residue_ref[:, cols] * jnp.sqrt(twice * series)
        taps = [[filter_ref[i, m : m + 1, cols] for m in range(3)] for i in range(3)]
        per_block = jnp.exp(-float(length) * decay)
        age0 = jnp.exp(-float(length - 1) * decay)
        age1 = jnp.exp(-float(length - 2) * decay)
        carry = jnp.zeros_like(decay)
        last = jnp.zeros((SUB, LANES), F32)
        for j in range(blocks - 1):
            there = given_ref[j].astype(F32)
            edge = there[at + h * SUB : at + (h + 1) * SUB]
            zero, one = first_signals(taps[1], taps[2], edge, last)
            gone = there[h * modes : (h + 1) * modes] + age0 * zero + age1 * one
            carry = jnp.where(j < place, per_block * carry + gone, carry)
            last = edge
        rows = slice(at + h * SUB, at + (h + 1) * SUB)
        firsts = first_signals(taps[1], taps[2], own[rows], before[rows])
        q_last = before[at + 2 * SUB + 2 * h : at + 2 * SUB + 2 * h + 2]
        q_more = [taps[0][1] * q_last[1:2] + taps[0][2] * q_last[0:1], taps[0][2] * q_last[1:2]]
        rate = [spread(decay[m : m + 1]) for m in range(modes)]
        keep = [jnp.exp(-r) for r in rate]
        state = []
        for m in range(modes):
            end = ends_ref[m, :, cols]
            more = jnp.exp(-float(steps - 1) * decay[m : m + 1]) * firsts[0]
            more = more + jnp.exp(-float(steps - 2) * decay[m : m + 1]) * firsts[1]
            end = jnp.where(chunk_id == 0, end + spread(more), end)
            run = jnp.where(chunk_id == 0, spread(carry[m : m + 1]), pltpu.roll(end, 1, 0))
            for far in (1, 2, 4):
                moved = jnp.where(chunk_id >= far, pltpu.roll(run, far, 0), 0.0)
                run = run + jnp.exp(-float(steps * far) * rate[m]) * moved
            state.append(run)
        gain = [spread(weight[m : m + 1]) for m in range(modes)]
        skip = spread(skip_ref[0:1, cols])
        for p in range(steps):
            if p % 2 == 0:
                signals = signal_ref[p // 2, :, cols].astype(F32)
                queries = query_ref[p // 2, :, cols].astype(F32)
            signal = signals[p % 2 * SUB : (p % 2 + 1) * SUB]
            query = queries[p % 2 * SUB : (p % 2 + 1) * SUB]
            if p < 2:
                signal = jnp.where(chunk_id == 0, spread(firsts[p]), signal)
                full = (first_ref[p, :, cols] + spread(q_more[p])).astype(BF16).astype(F32)
                query = jnp.where(chunk_id == 0, full, query)
            state = [keep[m] * state[m] + signal for m in range(modes)]
            terms = [gain[m] * state[m] for m in range(modes)]
            while len(terms) > 1:
                terms = [a + b for a, b in zip(terms[::2], terms[1::2])]
            conv = terms[0].astype(BF16).astype(F32)
            line_ref[h, pl.ds(p, SUB, stride=steps), :] = query * (conv + skip * signal)
        gated_ref[:, cols] = line_ref[h].astype(BF16)


def roll_kernel(place_ref, w_ref, *refs):
    outs, sems = refs[:-1], refs[-1]
    inner = w_ref.shape[1]
    copies = [
        pltpu.make_async_copy(w_ref.at[:, lax.rem(place_ref[0] + k, inner)], out, sems.at[k])
        for k, out in enumerate(outs)
    ]
    for copy in copies:
        copy.start()
    for copy in copies:
        copy.wait()


def mix_kernel(place_ref, gated_ref, own_ref, *refs):
    w_refs, part_ref = (own_ref,) + refs[:-1], refs[-1]
    inner = part_ref.shape[0]
    for k, w_ref in enumerate(w_refs):
        part_ref[lax.rem(place_ref[0] - k + inner, inner)] = sum(
            jnp.dot(gated_ref[z], w_ref[z], preferred_element_type=F32)
            for z in range(gated_ref.shape[0])
        ).astype(BF16)


def sum_kernel(part_ref, out_ref):
    total = part_ref[0].astype(F32)
    for k in range(1, part_ref.shape[0]):
        total = total + part_ref[k].astype(F32)
    out_ref[...] = total.astype(BF16)


def per_device(outer, proj, short_filter, residues, decays, skip, w_out):
    _, width, length = proj.shape
    modes = decays.shape[1]
    features = w_out.shape[1]
    blocks = lax.axis_size("ctx")
    groups = lax.axis_size("ch")
    inner = groups // outer
    steps = length // SUB
    shape = jax.ShapeDtypeStruct

    along_outer = [[a * inner + b for a in range(outer)] for b in range(inner)]
    along_inner = [[a * inner + b for b in range(inner)] for a in range(outer)]
    decays, residues = decays.T, residues.T
    short_filter = short_filter.swapaxes(1, 2)
    place = lax.axis_index("ctx").astype(jnp.int32).reshape(1)
    place_y = lax.rem(lax.axis_index("ch"), inner).astype(jnp.int32).reshape(1)
    whole = pl.BlockSpec(memory_space=pltpu.VMEM)
    scalar = pl.BlockSpec(memory_space=pltpu.SMEM)
    far = pl.BlockSpec(memory_space=pl.ANY)

    def full(*dims):
        return pl.BlockSpec(dims, lambda i: (0,) * len(dims))

    def one(i, lanes, at):
        return pl.BlockSpec((1, width, lanes), lambda g: (i, 0, at))

    sent_rows = 2 * modes + 3 * SUB
    sent, signal, query, first, ends = pallas(
        state_kernel,
        (
            shape((blocks, sent_rows, LANES), BF16),
            shape((steps // 2, 2 * SUB, width), BF16),
            shape((steps // 2, 2 * SUB, width), BF16),
            shape((2, SUB, width), F32),
            shape((modes, SUB, width), F32),
        ),
        (
            pltpu.VMEM((3, width // LANES, SUB + length, LANES), F32),
            pltpu.VMEM((sent_rows, LANES), F32),
        ),
        vmem=VMEM_WHOLE,
        grid=(1,),
        in_specs=[one(i, length, 0) for i in range(3)] + [full(3, 3, width), full(modes, width)],
        out_specs=[
            full(blocks, sent_rows, LANES),
            full(steps // 2, 2 * SUB, width),
            full(steps // 2, 2 * SUB, width),
            full(2, SUB, width),
            full(modes, SUB, width),
        ],
    )(proj, proj, proj, short_filter, decays)
    given = lax.all_to_all(sent, "ctx", 0, 0)
    w_parts = w_out.reshape(outer, inner, width, features)
    place_after, sent = lax.optimization_barrier((place_y, sent))
    rolled = pallas(
        roll_kernel,
        [shape((outer, width, features), BF16)] * inner,
        (pltpu.SemaphoreType.DMA((inner,)),),
        in_specs=[scalar, whole],
        out_specs=[whole] + [far] * (inner - 1),
    )(place_after, w_parts)
    w_near = [
        lax.ppermute(
            part, "ch",
            [(a * inner + b, a * inner + (b + k + 1) % inner) for a in range(outer) for b in range(inner)],
        )
        for k, part in enumerate(rolled[1:])
    ]
    gated = pallas(
        gate_kernel,
        shape((length, width), BF16),
        (pltpu.VMEM((width // LANES, length, LANES), F32),),
        in_specs=[scalar] + [whole] * 9,
    )(place, given, signal, query, first, ends, short_filter, decays, residues, skip.reshape(1, width))
    near = lax.all_gather(gated, "ch", axis_index_groups=along_outer)
    parts = pallas(
        mix_kernel,
        shape((inner, length, features), BF16),
        in_specs=[scalar] + [whole] * (1 + inner),
    )(place_y, near, rolled[0], *w_near)
    parts = lax.all_to_all(parts, "ch", 0, 0, axis_index_groups=along_inner)
    return pallas(sum_kernel, shape((length, features), BF16), in_specs=[whole])(parts)


def solution(mesh):
    groups = mesh.shape["ch"]
    outer = 4 if groups % 4 == 0 else 1
    in_specs = (
        P(None, "ch", "ctx"),
        P(None, "ch", None),
        P("ch", None),
        P("ch", None),
        P("ch"),
        P(None, "ch"),
    )
    return jax.shard_map(
        functools.partial(per_device, outer),
        mesh=mesh,
        in_specs=in_specs,
        out_specs=P("ctx", "ch"),
        check_vma=False,
    )
```

```python
import functools

import jax
import jax.numpy as jnp
from jax import lax
from jax.experimental import pallas as pl
from jax.experimental.pallas import tpu as pltpu
from jax.sharding import PartitionSpec as P

F32 = jnp.float32
BF16 = jnp.bfloat16
LANES = 128
SUB = 8
VMEM_LIMIT = 16 * 1024 * 1024
VMEM_WHOLE = 63 * 1024 * 1024


def pallas(body, out_shape, scratch=(), vmem=VMEM_LIMIT, **kwargs):
    return pl.pallas_call(
        body,
        out_shape=out_shape,
        scratch_shapes=list(scratch),
        compiler_params=pltpu.CompilerParams(vmem_limit_bytes=vmem),
        **kwargs,
    )


def halves(width):
    return [slice(lo, lo + LANES) for lo in range(0, width, LANES)]


def spread(row):
    return jnp.broadcast_to(row, (SUB, LANES))


def fill_line(line_ref, at, block):
    for h, cols in enumerate(halves(block.shape[1])):
        line_ref[at, h, :SUB, :] = jnp.zeros((SUB, LANES), F32)
        line_ref[at, h, SUB:, :] = block[:, cols]


def short_mix(line_ref, at, h, tap, steps):
    def rows(step):
        return line_ref[at, h, pl.ds(SUB + step, SUB, stride=steps), :]

    back2, back1 = rows(-2), rows(-1)
    for p in range(steps):
        here = rows(p)
        yield tap[0] * here + tap[1] * back1 + tap[2] * back2
        back2, back1 = back1, here


def signal_steps(k_line, v_line, filter_ref, h, cols, steps):
    chunk_id = lax.broadcasted_iota(jnp.int32, (SUB, LANES), 0)
    mixes = [
        short_mix(line_ref, at, h, [spread(filter_ref[i, m : m + 1, cols]) for m in range(3)], steps)
        for i, (line_ref, at) in enumerate((k_line, v_line), start=1)
    ]
    for p, (k, v) in enumerate(zip(*mixes)):
        signal = (k * v).astype(BF16).astype(F32)
        yield jnp.where(chunk_id == 0, 0.0, signal) if p < 2 else signal


def state_kernel(
    q_ref, k_ref, v_ref, filter_ref, decay_ref,
    sent_ref, signal_ref, query_ref, first_ref, ends_ref,
    line_ref, sums_ref,
):
    width, length = k_ref.shape[1:]
    steps = length // SUB
    modes = decay_ref.shape[0]
    blocks = [ref[0].astype(F32).T for ref in (q_ref, k_ref, v_ref)]
    for i, block in enumerate(blocks):
        fill_line(line_ref, i, block)
    chunk_id = lax.broadcasted_iota(jnp.int32, (SUB, LANES), 0)
    from_end = float(steps) * (SUB - 1 - chunk_id).astype(F32)
    for h, cols in enumerate(halves(width)):
        rate = [spread(decay_ref[m : m + 1, cols]) for m in range(modes)]
        keep = [jnp.exp(-r) for r in rate]
        state = [jnp.zeros((SUB, LANES), F32) for _ in range(modes)]
        pair = []
        for p, signal in enumerate(signal_steps((line_ref, 1), (line_ref, 2), filter_ref, h, cols, steps)):
            pair.append(signal)
            if p % 2:
                signal_ref[p // 2, :, cols] = jnp.concatenate(pair, axis=0).astype(BF16)
                pair = []
            state = [keep[m] * state[m] + signal for m in range(modes)]
        for m in range(modes):
            ends_ref[m, :, cols] = state[m]
            weight = jnp.exp(-rate[m] * from_end)
            sums_ref[h * modes + m : h * modes + m + 1, :] = jnp.sum(weight * state[m], axis=0, keepdims=True)
        tap = [spread(filter_ref[0, m : m + 1, cols]) for m in range(3)]
        mixes = list(short_mix(line_ref, 0, h, tap, steps))
        first_ref[0, :, cols], first_ref[1, :, cols] = mixes[:2]
        for p in range(0, steps, 2):
            query_ref[p // 2, :, cols] = jnp.concatenate(mixes[p : p + 2], axis=0).astype(BF16)
    edges = [blocks[1][-2:], blocks[2][-2:], blocks[1][:2], blocks[2][:2]]
    at = 2 * modes
    for h, cols in enumerate(halves(width)):
        for e, edge in enumerate(edges):
            sums_ref[at + h * SUB + 2 * e : at + h * SUB + 2 * e + 2, :] = edge[:, cols]
        sums_ref[at + 2 * SUB + 2 * h : at + 2 * SUB + 2 * h + 2, :] = blocks[0][-2:, cols]
    sums_ref[at + 2 * SUB + 4 :, :] = jnp.zeros((4, LANES), F32)
    sent = sums_ref[...].astype(BF16)
    for j in range(sent_ref.shape[0]):
        sent_ref[j] = sent


def first_signals(taps_k, taps_v, edge, last):
    def mixed(tap, first, before):
        zero = tap[0] * first[0:1] + tap[1] * before[1:2] + tap[2] * before[0:1]
        one = tap[0] * first[1:2] + tap[1] * first[0:1] + tap[2] * before[1:2]
        return zero, one

    k = mixed(taps_k, edge[4:6], last[0:2])
    v = mixed(taps_v, edge[6:8], last[2:4])
    return [(a * b).astype(BF16).astype(F32) for a, b in zip(k, v)]


def gate_kernel(
    place_ref, given_ref, signal_ref, query_ref, first_ref, ends_ref, filter_ref, decay_ref, residue_ref, skip_ref,
    gated_ref,
    line_ref,
):
    blocks = given_ref.shape[0]
    modes, width = decay_ref.shape
    steps = 2 * signal_ref.shape[0]
    length = steps * SUB
    at = 2 * modes
    place = place_ref[0]
    chunk_id = lax.broadcasted_iota(jnp.int32, (SUB, LANES), 0)
    own = given_ref[place].astype(F32)
    before = given_ref[jnp.maximum(place - 1, 0)].astype(F32)
    before = jnp.where(place > 0, before, 0.0)
    for h, cols in enumerate(halves(width)):
        decay = decay_ref[:, cols]
        twice = 2.0 * decay
        series = jnp.ones_like(twice)
        for n in (8, 7, 6, 5, 4, 3, 2):
            series = 1.0 - twice * (1.0 / n) * series
        weight = residue_ref[:, cols] * jnp.sqrt(twice * series)
        taps = [[filter_ref[i, m : m + 1, cols] for m in range(3)] for i in range(3)]
        per_block = jnp.exp(-float(length) * decay)
        age0 = jnp.exp(-float(length - 1) * decay)
        age1 = jnp.exp(-float(length - 2) * decay)
        carry = jnp.zeros_like(decay)
        last = jnp.zeros((SUB, LANES), F32)
        for j in range(blocks - 1):
            there = given_ref[j].astype(F32)
            edge = there[at + h * SUB : at + (h + 1) * SUB]
            zero, one = first_signals(taps[1], taps[2], edge, last)
            gone = there[h * modes : (h + 1) * modes] + age0 * zero + age1 * one
            carry = jnp.where(j < place, per_block * carry + gone, carry)
            last = edge
        rows = slice(at + h * SUB, at + (h + 1) * SUB)
        firsts = first_signals(taps[1], taps[2], own[rows], before[rows])
        q_last = before[at + 2 * SUB + 2 * h : at + 2 * SUB + 2 * h + 2]
        q_more = [taps[0][1] * q_last[1:2] + taps[0][2] * q_last[0:1], taps[0][2] * q_last[1:2]]
        rate = [spread(decay[m : m + 1]) for m in range(modes)]
        keep = [jnp.exp(-r) for r in rate]
        state = []
        for m in range(modes):
            end = ends_ref[m, :, cols]
            more = jnp.exp(-float(steps - 1) * decay[m : m + 1]) * firsts[0]
            more = more + jnp.exp(-float(steps - 2) * decay[m : m + 1]) * firsts[1]
            end = jnp.where(chunk_id == 0, end + spread(more), end)
            run = jnp.where(chunk_id == 0, spread(carry[m : m + 1]), pltpu.roll(end, 1, 0))
            for far in (1, 2, 4):
                moved = jnp.where(chunk_id >= far, pltpu.roll(run, far, 0), 0.0)
                run = run + jnp.exp(-float(steps * far) * rate[m]) * moved
            state.append(run)
        gain = [spread(weight[m : m + 1]) for m in range(modes)]
        skip = spread(skip_ref[0:1, cols])
        for p in range(steps):
            if p % 2 == 0:
                signals = signal_ref[p // 2, :, cols].astype(F32)
                queries = query_ref[p // 2, :, cols].astype(F32)
            signal = signals[p % 2 * SUB : (p % 2 + 1) * SUB]
            query = queries[p % 2 * SUB : (p % 2 + 1) * SUB]
            if p < 2:
                signal = jnp.where(chunk_id == 0, spread(firsts[p]), signal)
                full = (first_ref[p, :, cols] + spread(q_more[p])).astype(BF16).astype(F32)
                query = jnp.where(chunk_id == 0, full, query)
            state = [keep[m] * state[m] + signal for m in range(modes)]
            terms = [gain[m] * state[m] for m in range(modes)]
            while len(terms) > 1:
                terms = [a + b for a, b in zip(terms[::2], terms[1::2])]
            conv = terms[0].astype(BF16).astype(F32)
            line_ref[h, pl.ds(p, SUB, stride=steps), :] = query * (conv + skip * signal)
        gated_ref[:, cols] = line_ref[h].astype(BF16)


def roll_kernel(place_ref, w_ref, *refs):
    outs, sems = refs[:-1], refs[-1]
    outer, inner = w_ref.shape[:2]
    most, start = outer - 1, place_ref[1]
    copies = []
    for k, out in enumerate(outs):
        y = lax.rem(place_ref[0] + k, inner)
        copies.append(
            pltpu.make_async_copy(w_ref.at[pl.ds(start, most), y], out.at[pl.ds(0, most)], sems.at[k, 0])
        )
        copies.append(pltpu.make_async_copy(w_ref.at[lax.rem(start + most, outer), y], out.at[most], sems.at[k, 1]))
    for copy in copies:
        copy.start()
    for copy in copies:
        copy.wait()


def mix_kernel(place_ref, gated_ref, own_ref, *refs):
    w_refs, part_ref = (own_ref,) + refs[:-1], refs[-1]
    inner = part_ref.shape[0]
    for k, w_ref in enumerate(w_refs):
        part_ref[lax.rem(place_ref[0] - k + inner, inner)] = sum(
            jnp.dot(gated_ref[z], w_ref[z], preferred_element_type=F32)
            for z in range(gated_ref.shape[0])
        ).astype(BF16)


def sum_kernel(part_ref, out_ref):
    total = part_ref[0].astype(F32)
    for k in range(1, part_ref.shape[0]):
        total = total + part_ref[k].astype(F32)
    out_ref[...] = total.astype(BF16)


def per_device(outer, proj, short_filter, residues, decays, skip, w_out):
    _, width, length = proj.shape
    modes = decays.shape[1]
    features = w_out.shape[1]
    blocks = lax.axis_size("ctx")
    groups = lax.axis_size("ch")
    inner = groups // outer
    steps = length // SUB
    shape = jax.ShapeDtypeStruct

    along_inner = [[a * inner + b for b in range(inner)] for a in range(outer)]
    from_zero = ([0, 1], [2, 3]), ([0, 3], [1, 2])
    from_one = ([1, 2], [3, 0]), ([1, 0], [2, 3])
    turns = (from_one, from_zero)

    def rings(turn):
        return [
            [i * groups + a * inner + b for a in pair]
            for i in range(blocks)
            for b in range(inner)
            for pair in turns[i % 2][turn]
        ]

    odd = lax.rem(lax.axis_index("ctx"), 2)
    decays, residues = decays.T, residues.T
    short_filter = short_filter.swapaxes(1, 2)
    place = lax.axis_index("ctx").astype(jnp.int32).reshape(1)
    place_y = lax.rem(lax.axis_index("ch"), inner).astype(jnp.int32).reshape(1)
    whole = pl.BlockSpec(memory_space=pltpu.VMEM)
    scalar = pl.BlockSpec(memory_space=pltpu.SMEM)
    far = pl.BlockSpec(memory_space=pl.ANY)

    def full(*dims):
        return pl.BlockSpec(dims, lambda i: (0,) * len(dims))

    def one(i, lanes, at):
        return pl.BlockSpec((1, width, lanes), lambda g: (i, 0, at))

    sent_rows = 2 * modes + 3 * SUB
    sent, signal, query, first, ends = pallas(
        state_kernel,
        (
            shape((blocks, sent_rows, LANES), BF16),
            shape((steps // 2, 2 * SUB, width), BF16),
            shape((steps // 2, 2 * SUB, width), BF16),
            shape((2, SUB, width), F32),
            shape((modes, SUB, width), F32),
        ),
        (
            pltpu.VMEM((3, width // LANES, SUB + length, LANES), F32),
            pltpu.VMEM((sent_rows, LANES), F32),
        ),
        vmem=VMEM_WHOLE,
        grid=(1,),
        in_specs=[one(i, length, 0) for i in range(3)] + [full(3, 3, width), full(modes, width)],
        out_specs=[
            full(blocks, sent_rows, LANES),
            full(steps // 2, 2 * SUB, width),
            full(steps // 2, 2 * SUB, width),
            full(2, SUB, width),
            full(modes, SUB, width),
        ],
    )(proj, proj, proj, short_filter, decays)
    given = lax.all_to_all(sent, "ctx", 0, 0)
    w_parts = w_out.reshape(outer, inner, width, features)
    spots = jnp.stack([place_y[0], 1 - odd]).astype(jnp.int32)
    spots, sent = lax.optimization_barrier((spots, sent))
    rolled = pallas(
        roll_kernel,
        [shape((outer, width, features), BF16)] * inner,
        (pltpu.SemaphoreType.DMA((inner, 2)),),
        in_specs=[scalar, whole],
        out_specs=[whole] + [far] * (inner - 1),
    )(spots, w_parts)
    w_near = [
        lax.ppermute(
            part, "ch",
            [(a * inner + b, a * inner + (b + k + 1) % inner) for a in range(outer) for b in range(inner)],
        )
        for k, part in enumerate(rolled[1:])
    ]
    gated = pallas(
        gate_kernel,
        shape((length, width), BF16),
        (pltpu.VMEM((width // LANES, length, LANES), F32),),
        in_specs=[scalar] + [whole] * 9,
    )(place, given, signal, query, first, ends, short_filter, decays, residues, skip.reshape(1, width))
    near = lax.all_gather(gated, ("ctx", "ch"), axis_index_groups=rings(0))
    near = lax.all_gather(near, ("ctx", "ch"), axis_index_groups=rings(1)).reshape(outer, length, width)
    parts = pallas(
        mix_kernel,
        shape((inner, length, features), BF16),
        in_specs=[scalar] + [whole] * (1 + inner),
    )(place_y, near, rolled[0], *w_near)
    parts = lax.all_to_all(parts, "ch", 0, 0, axis_index_groups=along_inner)
    return pallas(sum_kernel, shape((length, features), BF16), in_specs=[whole])(parts)


def solution(mesh):
    groups = mesh.shape["ch"]
    outer = 4 if groups % 4 == 0 else 1
    in_specs = (
        P(None, "ch", "ctx"),
        P(None, "ch", None),
        P("ch", None),
        P("ch", None),
        P("ch"),
        P(None, "ch"),
    )
    return jax.shard_map(
        functools.partial(per_device, outer),
        mesh=mesh,
        in_specs=in_specs,
        out_specs=P("ctx", "ch"),
        check_vma=False,
    )
```

```python
import functools

import jax
import jax.numpy as jnp
from jax import lax
from jax.experimental import pallas as pl
from jax.experimental.pallas import tpu as pltpu
from jax.sharding import PartitionSpec as P

F32 = jnp.float32
BF16 = jnp.bfloat16
LANES = 128
SUB = 8
VMEM_LIMIT = 16 * 1024 * 1024
VMEM_WHOLE = 63 * 1024 * 1024


def pallas(body, out_shape, scratch=(), vmem=VMEM_LIMIT, **kwargs):
    return pl.pallas_call(
        body,
        out_shape=out_shape,
        scratch_shapes=list(scratch),
        compiler_params=pltpu.CompilerParams(vmem_limit_bytes=vmem),
        **kwargs,
    )


def halves(width):
    return [slice(lo, lo + LANES) for lo in range(0, width, LANES)]


def spread(row):
    return jnp.broadcast_to(row, (SUB, LANES))


def fill_line(line_ref, at, block):
    for h, cols in enumerate(halves(block.shape[1])):
        line_ref[at, h, :SUB, :] = jnp.zeros((SUB, LANES), F32)
        line_ref[at, h, SUB:, :] = block[:, cols]


def short_mix(line_ref, at, h, tap, steps):
    def rows(step):
        return line_ref[at, h, pl.ds(SUB + step, SUB, stride=steps), :]

    back2, back1 = rows(-2), rows(-1)
    for p in range(steps):
        here = rows(p)
        yield tap[0] * here + tap[1] * back1 + tap[2] * back2
        back2, back1 = back1, here


def signal_steps(k_line, v_line, filter_ref, h, cols, steps):
    chunk_id = lax.broadcasted_iota(jnp.int32, (SUB, LANES), 0)
    mixes = [
        short_mix(line_ref, at, h, [spread(filter_ref[i, m : m + 1, cols]) for m in range(3)], steps)
        for i, (line_ref, at) in enumerate((k_line, v_line), start=1)
    ]
    for p, (k, v) in enumerate(zip(*mixes)):
        signal = (k * v).astype(BF16).astype(F32)
        yield jnp.where(chunk_id == 0, 0.0, signal) if p < 2 else signal


def state_kernel(
    q_ref, k_ref, v_ref, filter_ref, decay_ref,
    sent_ref, signal_ref, query_ref, first_ref, ends_ref,
    line_ref, sums_ref,
):
    width, length = k_ref.shape[1:]
    steps = length // SUB
    modes = decay_ref.shape[0]
    blocks = [ref[0].T.astype(F32) for ref in (q_ref, k_ref, v_ref)]
    for i, block in enumerate(blocks):
        fill_line(line_ref, i, block)
    chunk_id = lax.broadcasted_iota(jnp.int32, (SUB, LANES), 0)
    from_end = float(steps) * (SUB - 1 - chunk_id).astype(F32)
    for h, cols in enumerate(halves(width)):
        rate = [spread(decay_ref[m : m + 1, cols]) for m in range(modes)]
        keep = [jnp.exp(-r) for r in rate]
        state = [jnp.zeros((SUB, LANES), F32) for _ in range(modes)]
        pair = []
        for p, signal in enumerate(signal_steps((line_ref, 1), (line_ref, 2), filter_ref, h, cols, steps)):
            pair.append(signal)
            if p % 2:
                signal_ref[p // 2, :, cols] = jnp.concatenate(pair, axis=0).astype(BF16)
                pair = []
            state = [keep[m] * state[m] + signal for m in range(modes)]
        for m in range(modes):
            ends_ref[m, :, cols] = state[m]
            weight = jnp.exp(-rate[m] * from_end)
            sums_ref[h * modes + m : h * modes + m + 1, :] = jnp.sum(weight * state[m], axis=0, keepdims=True)
        tap = [spread(filter_ref[0, m : m + 1, cols]) for m in range(3)]
        mixes = list(short_mix(line_ref, 0, h, tap, steps))
        first_ref[0, :, cols], first_ref[1, :, cols] = mixes[:2]
        for p in range(0, steps, 2):
            query_ref[p // 2, :, cols] = jnp.concatenate(mixes[p : p + 2], axis=0).astype(BF16)
    edges = [blocks[1][-2:], blocks[2][-2:], blocks[1][:2], blocks[2][:2]]
    at = 2 * modes
    for h, cols in enumerate(halves(width)):
        for e, edge in enumerate(edges):
            for r in range(2):
                row = at + 2 * (2 * e + r) + h
                sums_ref[row : row + 1, :] = edge[r : r + 1, cols]
        sums_ref[at + 2 * SUB + 2 * h : at + 2 * SUB + 2 * h + 2, :] = blocks[0][-2:, cols]
    sums_ref[at + 2 * SUB + 4 :, :] = jnp.zeros((4, LANES), F32)
    sent = sums_ref[...].astype(BF16)
    for j in range(sent_ref.shape[0]):
        sent_ref[j] = sent


def first_signals(taps_k, taps_v, edge, last):
    def item(rows, n):
        return rows[2 * n : 2 * n + 2]

    def mixed(tap, n):
        before2, before1, here, after = item(last, n), item(last, n + 1), item(edge, n + 4), item(edge, n + 5)
        zero = tap[0] * here + tap[1] * before1 + tap[2] * before2
        one = tap[0] * after + tap[1] * here + tap[2] * before1
        return zero, one

    return [(a * b).astype(BF16).astype(F32) for a, b in zip(mixed(taps_k, 0), mixed(taps_v, 2))]


def gate_kernel(
    place_ref, given_ref, signal_ref, query_ref, first_ref, ends_ref, filter_ref, decay_ref, residue_ref, skip_ref,
    gated_ref,
    line_ref,
):
    blocks = given_ref.shape[0]
    modes, width = decay_ref.shape
    steps = 2 * signal_ref.shape[0]
    length = steps * SUB
    at = 2 * modes
    place = place_ref[0]
    chunk_id = lax.broadcasted_iota(jnp.int32, (SUB, LANES), 0)
    own = given_ref[place].astype(F32)
    before = given_ref[jnp.maximum(place - 1, 0)].astype(F32)
    before = jnp.where(place > 0, before, 0.0)
    parts = halves(width)
    rows = slice(at, at + 2 * SUB)
    both = [[jnp.concatenate([filter_ref[i, m : m + 1, cols] for cols in parts], 0) for m in range(3)] for i in (1, 2)]
    ages = [[jnp.exp(-float(length - n) * decay_ref[:, cols]) for cols in parts] for n in range(3)]
    carries = [jnp.zeros((modes, LANES), F32) for _ in parts]
    last = jnp.zeros((2 * SUB, LANES), F32)
    for j in range(blocks - 1):
        there = given_ref[j].astype(F32)
        edge = there[rows]
        zero, one = first_signals(*both, edge, last)
        for h in range(2):
            gone = there[h * modes : (h + 1) * modes] + ages[1][h] * zero[h : h + 1] + ages[2][h] * one[h : h + 1]
            carries[h] = jnp.where(j < place, ages[0][h] * carries[h] + gone, carries[h])
        last = edge
    own_first = first_signals(*both, own[rows], before[rows])
    for h, cols in enumerate(parts):
        decay = decay_ref[:, cols]
        twice = 2.0 * decay
        series = jnp.ones_like(twice)
        for n in (8, 7, 6, 5, 4, 3, 2):
            series = 1.0 - twice * (1.0 / n) * series
        weight = residue_ref[:, cols] * jnp.sqrt(twice * series)
        carry = carries[h]
        firsts = [f[h : h + 1] for f in own_first]
        tap = [filter_ref[0, m : m + 1, cols] for m in range(3)]
        q_last = before[at + 2 * SUB + 2 * h : at + 2 * SUB + 2 * h + 2]
        q_more = [tap[1] * q_last[1:2] + tap[2] * q_last[0:1], tap[2] * q_last[1:2]]
        rate = [spread(decay[m : m + 1]) for m in range(modes)]
        keep = [jnp.exp(-r) for r in rate]
        state = []
        for m in range(modes):
            end = ends_ref[m, :, cols]
            more = jnp.exp(-float(steps - 1) * decay[m : m + 1]) * firsts[0]
            more = more + jnp.exp(-float(steps - 2) * decay[m : m + 1]) * firsts[1]
            end = jnp.where(chunk_id == 0, end + spread(more), end)
            run = jnp.where(chunk_id == 0, spread(carry[m : m + 1]), pltpu.roll(end, 1, 0))
            for far in (1, 2, 4):
                moved = jnp.where(chunk_id >= far, pltpu.roll(run, far, 0), 0.0)
                run = run + jnp.exp(-float(steps * far) * rate[m]) * moved
            state.append(run)
        gain = [spread(weight[m : m + 1]) for m in range(modes)]
        skip = spread(skip_ref[0:1, cols])
        for p in range(steps):
            if p % 2 == 0:
                signals = signal_ref[p // 2, :, cols].astype(F32)
                queries = query_ref[p // 2, :, cols].astype(F32)
            signal = signals[p % 2 * SUB : (p % 2 + 1) * SUB]
            query = queries[p % 2 * SUB : (p % 2 + 1) * SUB]
            if p < 2:
                signal = jnp.where(chunk_id == 0, spread(firsts[p]), signal)
                full = (first_ref[p, :, cols] + spread(q_more[p])).astype(BF16).astype(F32)
                query = jnp.where(chunk_id == 0, full, query)
            state = [keep[m] * state[m] + signal for m in range(modes)]
            terms = [gain[m] * state[m] for m in range(modes)]
            while len(terms) > 1:
                terms = [a + b for a, b in zip(terms[::2], terms[1::2])]
            conv = terms[0].astype(BF16).astype(F32)
            line_ref[h, pl.ds(p, SUB, stride=steps), :] = query * (conv + skip * signal)
        gated_ref[:, cols] = line_ref[h].astype(BF16)


def roll_kernel(place_ref, w_ref, *refs):
    outs, sems = refs[:-1], refs[-1]
    outer, inner = w_ref.shape[:2]
    most, start = outer - 1, place_ref[1]
    copies = []
    for k, out in enumerate(outs):
        y = lax.rem(place_ref[0] + k, inner)
        copies.append(
            pltpu.make_async_copy(w_ref.at[pl.ds(start, most), y], out.at[pl.ds(0, most)], sems.at[k, 0])
        )
        copies.append(pltpu.make_async_copy(w_ref.at[lax.rem(start + most, outer), y], out.at[most], sems.at[k, 1]))
    for copy in copies:
        copy.start()
    for copy in copies:
        copy.wait()


def mix_kernel(place_ref, gated_ref, own_ref, *refs):
    w_refs, part_ref = (own_ref,) + refs[:-1], refs[-1]
    inner = part_ref.shape[0]
    for k, w_ref in enumerate(w_refs):
        part_ref[lax.rem(place_ref[0] - k + inner, inner)] = sum(
            jnp.dot(gated_ref[z], w_ref[z], preferred_element_type=F32)
            for z in range(gated_ref.shape[0])
        ).astype(BF16)


def sum_kernel(part_ref, out_ref):
    total = part_ref[0].astype(F32)
    for k in range(1, part_ref.shape[0]):
        total = total + part_ref[k].astype(F32)
    out_ref[...] = total.astype(BF16)


def per_device(outer, proj, short_filter, residues, decays, skip, w_out):
    _, width, length = proj.shape
    modes = decays.shape[1]
    features = w_out.shape[1]
    blocks = lax.axis_size("ctx")
    groups = lax.axis_size("ch")
    inner = groups // outer
    steps = length // SUB
    shape = jax.ShapeDtypeStruct

    along_inner = [[a * inner + b for b in range(inner)] for a in range(outer)]
    from_zero = ([0, 1], [2, 3]), ([0, 3], [1, 2])
    from_one = ([1, 2], [3, 0]), ([1, 0], [2, 3])
    turns = (from_one, from_zero)

    def rings(turn):
        return [
            [i * groups + a * inner + b for a in pair]
            for i in range(blocks)
            for b in range(inner)
            for pair in turns[i % 2][turn]
        ]

    odd = lax.rem(lax.axis_index("ctx"), 2)
    decays, residues = decays.T, residues.T
    short_filter = short_filter.swapaxes(1, 2)
    place = lax.axis_index("ctx").astype(jnp.int32).reshape(1)
    place_y = lax.rem(lax.axis_index("ch"), inner).astype(jnp.int32).reshape(1)
    whole = pl.BlockSpec(memory_space=pltpu.VMEM)
    scalar = pl.BlockSpec(memory_space=pltpu.SMEM)
    far = pl.BlockSpec(memory_space=pl.ANY)

    def full(*dims):
        return pl.BlockSpec(dims, lambda i: (0,) * len(dims))

    def one(i, lanes, at):
        return pl.BlockSpec((1, width, lanes), lambda g: (i, 0, at))

    sent_rows = 2 * modes + 3 * SUB
    sent, signal, query, first, ends = pallas(
        state_kernel,
        (
            shape((blocks, sent_rows, LANES), BF16),
            shape((steps // 2, 2 * SUB, width), BF16),
            shape((steps // 2, 2 * SUB, width), BF16),
            shape((2, SUB, width), F32),
            shape((modes, SUB, width), F32),
        ),
        (
            pltpu.VMEM((3, width // LANES, SUB + length, LANES), F32),
            pltpu.VMEM((sent_rows, LANES), F32),
        ),
        vmem=VMEM_WHOLE,
        grid=(1,),
        in_specs=[one(i, length, 0) for i in range(3)] + [full(3, 3, width), full(modes, width)],
        out_specs=[
            full(blocks, sent_rows, LANES),
            full(steps // 2, 2 * SUB, width),
            full(steps // 2, 2 * SUB, width),
            full(2, SUB, width),
            full(modes, SUB, width),
        ],
    )(proj, proj, proj, short_filter, decays)
    given = lax.all_to_all(sent, "ctx", 0, 0)
    w_parts = w_out.reshape(outer, inner, width, features)
    spots = jnp.stack([place_y[0], 1 - odd]).astype(jnp.int32)
    spots, sent = lax.optimization_barrier((spots, sent))
    rolled = pallas(
        roll_kernel,
        [shape((outer, width, features), BF16)] * inner,
        (pltpu.SemaphoreType.DMA((inner, 2)),),
        in_specs=[scalar, whole],
        out_specs=[whole] + [far] * (inner - 1),
    )(spots, w_parts)
    w_near = [
        lax.ppermute(
            part, "ch",
            [(a * inner + b, a * inner + (b + k + 1) % inner) for a in range(outer) for b in range(inner)],
        )
        for k, part in enumerate(rolled[1:])
    ]
    gated = pallas(
        gate_kernel,
        shape((length, width), BF16),
        (pltpu.VMEM((width // LANES, length, LANES), F32),),
        in_specs=[scalar] + [whole] * 9,
    )(place, given, signal, query, first, ends, short_filter, decays, residues, skip.reshape(1, width))
    near = lax.all_gather(gated, ("ctx", "ch"), axis_index_groups=rings(0))
    near = lax.all_gather(near, ("ctx", "ch"), axis_index_groups=rings(1)).reshape(outer, length, width)
    parts = pallas(
        mix_kernel,
        shape((inner, length, features), BF16),
        in_specs=[scalar] + [whole] * (1 + inner),
    )(place_y, near, rolled[0], *w_near)
    parts = lax.all_to_all(parts, "ch", 0, 0, axis_index_groups=along_inner)
    return pallas(sum_kernel, shape((length, features), BF16), in_specs=[whole])(parts)


def solution(mesh):
    groups = mesh.shape["ch"]
    outer = 4 if groups % 4 == 0 else 1
    in_specs = (
        P(None, "ch", "ctx"),
        P(None, "ch", None),
        P("ch", None),
        P("ch", None),
        P("ch"),
        P(None, "ch"),
    )
    return jax.shard_map(
        functools.partial(per_device, outer),
        mesh=mesh,
        in_specs=in_specs,
        out_specs=P("ctx", "ch"),
        check_vma=False,
    )
```

```python
import functools

import jax
import jax.numpy as jnp
from jax import lax
from jax.experimental import pallas as pl
from jax.experimental.pallas import tpu as pltpu
from jax.sharding import PartitionSpec as P

F32 = jnp.float32
BF16 = jnp.bfloat16
LANES = 128
SUB = 8
VMEM_LIMIT = 16 * 1024 * 1024
VMEM_WHOLE = 63 * 1024 * 1024


def pallas(body, out_shape, scratch=(), vmem=VMEM_LIMIT, **kwargs):
    return pl.pallas_call(
        body,
        out_shape=out_shape,
        scratch_shapes=list(scratch),
        compiler_params=pltpu.CompilerParams(vmem_limit_bytes=vmem),
        **kwargs,
    )


def halves(width):
    return [slice(lo, lo + LANES) for lo in range(0, width, LANES)]


def spread(row):
    return jnp.broadcast_to(row, (SUB, LANES))


def fill_line(line_ref, at, block):
    for h, cols in enumerate(halves(block.shape[1])):
        line_ref[at, h, :SUB, :] = jnp.zeros((SUB, LANES), F32)
        line_ref[at, h, SUB:, :] = block[:, cols]


def short_mix(line_ref, at, h, tap, steps):
    def rows(step):
        return line_ref[at, h, pl.ds(SUB + step, SUB, stride=steps), :]

    back2, back1 = rows(-2), rows(-1)
    for p in range(steps):
        here = rows(p)
        yield tap[0] * here + tap[1] * back1 + tap[2] * back2
        back2, back1 = back1, here


def signal_steps(k_line, v_line, filter_ref, h, cols, steps):
    chunk_id = lax.broadcasted_iota(jnp.int32, (SUB, LANES), 0)
    mixes = [
        short_mix(line_ref, at, h, [spread(filter_ref[i, m : m + 1, cols]) for m in range(3)], steps)
        for i, (line_ref, at) in enumerate((k_line, v_line), start=1)
    ]
    for p, (k, v) in enumerate(zip(*mixes)):
        signal = (k * v).astype(BF16).astype(F32)
        yield jnp.where(chunk_id == 0, 0.0, signal) if p < 2 else signal


def state_kernel(
    q_ref, k_ref, v_ref, filter_ref, decay_ref,
    sent_ref, signal_ref, query_ref, first_ref, ends_ref,
    line_ref, sums_ref,
):
    width, length = k_ref.shape[1:]
    steps = length // SUB
    modes = decay_ref.shape[0]
    blocks = [ref[0].T.astype(F32) for ref in (q_ref, k_ref, v_ref)]
    for i, block in enumerate(blocks):
        fill_line(line_ref, i, block)
    chunk_id = lax.broadcasted_iota(jnp.int32, (SUB, LANES), 0)
    from_end = float(steps) * (SUB - 1 - chunk_id).astype(F32)
    for h, cols in enumerate(halves(width)):
        rate = [spread(decay_ref[m : m + 1, cols]) for m in range(modes)]
        keep = [jnp.exp(-r) for r in rate]
        state = [jnp.zeros((SUB, LANES), F32) for _ in range(modes)]
        pair = []
        for p, signal in enumerate(signal_steps((line_ref, 1), (line_ref, 2), filter_ref, h, cols, steps)):
            pair.append(signal)
            if p % 2:
                signal_ref[p // 2, :, cols] = jnp.concatenate(pair, axis=0).astype(BF16)
                pair = []
            state = [keep[m] * state[m] + signal for m in range(modes)]
        for m in range(modes):
            ends_ref[m, :, cols] = state[m]
            weight = jnp.exp(-rate[m] * from_end)
            sums_ref[h * modes + m : h * modes + m + 1, :] = jnp.sum(weight * state[m], axis=0, keepdims=True)
        tap = [spread(filter_ref[0, m : m + 1, cols]) for m in range(3)]
        mixes = list(short_mix(line_ref, 0, h, tap, steps))
        first_ref[0, :, cols], first_ref[1, :, cols] = mixes[:2]
        for p in range(0, steps, 2):
            query_ref[p // 2, :, cols] = jnp.concatenate(mixes[p : p + 2], axis=0).astype(BF16)
    edges = [blocks[1][-2:], blocks[2][-2:], blocks[1][:2], blocks[2][:2]]
    at = 2 * modes
    for h, cols in enumerate(halves(width)):
        for e, edge in enumerate(edges):
            for r in range(2):
                row = at + 2 * (2 * e + r) + h
                sums_ref[row : row + 1, :] = edge[r : r + 1, cols]
        sums_ref[at + 2 * SUB + 2 * h : at + 2 * SUB + 2 * h + 2, :] = blocks[0][-2:, cols]
    sums_ref[at + 2 * SUB + 4 :, :] = jnp.zeros((4, LANES), F32)
    sent = sums_ref[...].astype(BF16)
    for j in range(sent_ref.shape[0]):
        sent_ref[j] = sent


def first_signals(taps_k, taps_v, edge, last):
    def item(rows, n):
        return rows[2 * n : 2 * n + 2]

    def mixed(tap, n):
        before2, before1, here, after = item(last, n), item(last, n + 1), item(edge, n + 4), item(edge, n + 5)
        zero = tap[0] * here + tap[1] * before1 + tap[2] * before2
        one = tap[0] * after + tap[1] * here + tap[2] * before1
        return zero, one

    return [(a * b).astype(BF16).astype(F32) for a, b in zip(mixed(taps_k, 0), mixed(taps_v, 2))]


def gate_kernel(
    place_ref, given_ref, signal_ref, query_ref, first_ref, ends_ref, filter_ref, decay_ref, residue_ref, skip_ref,
    gated_ref,
    line_ref,
):
    blocks = given_ref.shape[0]
    modes, width = decay_ref.shape
    steps = 2 * signal_ref.shape[0]
    length = steps * SUB
    at = 2 * modes
    place = place_ref[0]
    chunk_id = lax.broadcasted_iota(jnp.int32, (SUB, LANES), 0)
    own = given_ref[place].astype(F32)
    before = given_ref[jnp.maximum(place - 1, 0)].astype(F32)
    before = jnp.where(place > 0, before, 0.0)
    parts = halves(width)
    rows = slice(at, at + 2 * SUB)
    both = [[jnp.concatenate([filter_ref[i, m : m + 1, cols] for cols in parts], 0) for m in range(3)] for i in (1, 2)]
    ages = [[jnp.exp(-float(length - n) * decay_ref[:, cols]) for cols in parts] for n in range(3)]
    carries = [jnp.zeros((modes, LANES), F32) for _ in parts]
    last = jnp.zeros((2 * SUB, LANES), F32)
    for j in range(blocks - 1):
        there = given_ref[j].astype(F32)
        edge = there[rows]
        zero, one = first_signals(*both, edge, last)
        for h in range(2):
            gone = there[h * modes : (h + 1) * modes] + ages[1][h] * zero[h : h + 1] + ages[2][h] * one[h : h + 1]
            carries[h] = jnp.where(j < place, ages[0][h] * carries[h] + gone, carries[h])
        last = edge
    own_first = first_signals(*both, own[rows], before[rows])
    for h, cols in enumerate(parts):
        decay = decay_ref[:, cols]
        twice = 2.0 * decay
        series = jnp.ones_like(twice)
        for n in (8, 7, 6, 5, 4, 3, 2):
            series = 1.0 - twice * (1.0 / n) * series
        weight = residue_ref[:, cols] * jnp.sqrt(twice * series)
        carry = carries[h]
        firsts = [f[h : h + 1] for f in own_first]
        tap = [filter_ref[0, m : m + 1, cols] for m in range(3)]
        q_last = before[at + 2 * SUB + 2 * h : at + 2 * SUB + 2 * h + 2]
        q_more = [tap[1] * q_last[1:2] + tap[2] * q_last[0:1], tap[2] * q_last[1:2]]
        one_step = jnp.exp(-decay)
        one_chunk = jnp.exp(-float(steps) * decay)
        chunks = {1: one_chunk, 2: one_chunk * one_chunk}
        chunks[4] = chunks[2] * chunks[2]
        aged = [jnp.exp(-float(steps - 1 - n) * decay) for n in range(2)]
        keep = [spread(one_step[m : m + 1]) for m in range(modes)]
        state = []
        for m in range(modes):
            end = ends_ref[m, :, cols]
            more = aged[0][m : m + 1] * firsts[0] + aged[1][m : m + 1] * firsts[1]
            end = jnp.where(chunk_id == 0, end + spread(more), end)
            run = jnp.where(chunk_id == 0, spread(carry[m : m + 1]), pltpu.roll(end, 1, 0))
            for far in (1, 2, 4):
                moved = jnp.where(chunk_id >= far, pltpu.roll(run, far, 0), 0.0)
                run = run + spread(chunks[far][m : m + 1]) * moved
            state.append(run)
        gain = [spread(weight[m : m + 1]) for m in range(modes)]
        skip = spread(skip_ref[0:1, cols])
        for p in range(steps):
            if p % 2 == 0:
                signals = signal_ref[p // 2, :, cols].astype(F32)
                queries = query_ref[p // 2, :, cols].astype(F32)
            signal = signals[p % 2 * SUB : (p % 2 + 1) * SUB]
            query = queries[p % 2 * SUB : (p % 2 + 1) * SUB]
            if p < 2:
                signal = jnp.where(chunk_id == 0, spread(firsts[p]), signal)
                full = (first_ref[p, :, cols] + spread(q_more[p])).astype(BF16).astype(F32)
                query = jnp.where(chunk_id == 0, full, query)
            state = [keep[m] * state[m] + signal for m in range(modes)]
            terms = [gain[m] * state[m] for m in range(modes)]
            while len(terms) > 1:
                terms = [a + b for a, b in zip(terms[::2], terms[1::2])]
            conv = terms[0].astype(BF16).astype(F32)
            line_ref[h, pl.ds(p, SUB, stride=steps), :] = query * (conv + skip * signal)
        gated_ref[:, cols] = line_ref[h].astype(BF16)


def roll_kernel(place_ref, w_ref, *refs):
    outs, sems = refs[:-1], refs[-1]
    outer, inner = w_ref.shape[:2]
    most, start = outer - 1, place_ref[1]
    copies = []
    for k, out in enumerate(outs):
        y = lax.rem(place_ref[0] + k, inner)
        copies.append(
            pltpu.make_async_copy(w_ref.at[pl.ds(start, most), y], out.at[pl.ds(0, most)], sems.at[k, 0])
        )
        copies.append(pltpu.make_async_copy(w_ref.at[lax.rem(start + most, outer), y], out.at[most], sems.at[k, 1]))
    for copy in copies:
        copy.start()
    for copy in copies:
        copy.wait()


def mix_kernel(place_ref, gated_ref, own_ref, *refs):
    w_refs, part_ref = (own_ref,) + refs[:-1], refs[-1]
    inner = part_ref.shape[0]
    for k, w_ref in enumerate(w_refs):
        part_ref[lax.rem(place_ref[0] - k + inner, inner)] = sum(
            jnp.dot(gated_ref[z], w_ref[z], preferred_element_type=F32)
            for z in range(gated_ref.shape[0])
        ).astype(BF16)


def sum_kernel(part_ref, out_ref):
    total = part_ref[0].astype(F32)
    for k in range(1, part_ref.shape[0]):
        total = total + part_ref[k].astype(F32)
    out_ref[...] = total.astype(BF16)


def per_device(outer, proj, short_filter, residues, decays, skip, w_out):
    _, width, length = proj.shape
    modes = decays.shape[1]
    features = w_out.shape[1]
    blocks = lax.axis_size("ctx")
    groups = lax.axis_size("ch")
    inner = groups // outer
    steps = length // SUB
    shape = jax.ShapeDtypeStruct

    along_inner = [[a * inner + b for b in range(inner)] for a in range(outer)]
    from_zero = ([0, 1], [2, 3]), ([0, 3], [1, 2])
    from_one = ([1, 2], [3, 0]), ([1, 0], [2, 3])
    turns = (from_one, from_zero)

    def rings(turn):
        return [
            [i * groups + a * inner + b for a in pair]
            for i in range(blocks)
            for b in range(inner)
            for pair in turns[i % 2][turn]
        ]

    odd = lax.rem(lax.axis_index("ctx"), 2)
    decays, residues = decays.T, residues.T
    short_filter = short_filter.swapaxes(1, 2)
    place = lax.axis_index("ctx").astype(jnp.int32).reshape(1)
    place_y = lax.rem(lax.axis_index("ch"), inner).astype(jnp.int32).reshape(1)
    whole = pl.BlockSpec(memory_space=pltpu.VMEM)
    scalar = pl.BlockSpec(memory_space=pltpu.SMEM)
    far = pl.BlockSpec(memory_space=pl.ANY)

    def full(*dims):
        return pl.BlockSpec(dims, lambda i: (0,) * len(dims))

    def one(i, lanes, at):
        return pl.BlockSpec((1, width, lanes), lambda g: (i, 0, at))

    sent_rows = 2 * modes + 3 * SUB
    sent, signal, query, first, ends = pallas(
        state_kernel,
        (
            shape((blocks, sent_rows, LANES), BF16),
            shape((steps // 2, 2 * SUB, width), BF16),
            shape((steps // 2, 2 * SUB, width), BF16),
            shape((2, SUB, width), F32),
            shape((modes, SUB, width), F32),
        ),
        (
            pltpu.VMEM((3, width // LANES, SUB + length, LANES), F32),
            pltpu.VMEM((sent_rows, LANES), F32),
        ),
        vmem=VMEM_WHOLE,
        grid=(1,),
        in_specs=[one(i, length, 0) for i in range(3)] + [full(3, 3, width), full(modes, width)],
        out_specs=[
            full(blocks, sent_rows, LANES),
            full(steps // 2, 2 * SUB, width),
            full(steps // 2, 2 * SUB, width),
            full(2, SUB, width),
            full(modes, SUB, width),
        ],
    )(proj, proj, proj, short_filter, decays)
    given = lax.all_to_all(sent, "ctx", 0, 0)
    w_parts = w_out.reshape(outer, inner, width, features)
    spots = jnp.stack([place_y[0], 1 - odd]).astype(jnp.int32)
    spots, sent = lax.optimization_barrier((spots, sent))
    rolled = pallas(
        roll_kernel,
        [shape((outer, width, features), BF16)] * inner,
        (pltpu.SemaphoreType.DMA((inner, 2)),),
        in_specs=[scalar, whole],
        out_specs=[whole] + [far] * (inner - 1),
    )(spots, w_parts)
    w_near = [
        lax.ppermute(
            part, "ch",
            [(a * inner + b, a * inner + (b + k + 1) % inner) for a in range(outer) for b in range(inner)],
        )
        for k, part in enumerate(rolled[1:])
    ]
    gated = pallas(
        gate_kernel,
        shape((length, width), BF16),
        (pltpu.VMEM((width // LANES, length, LANES), F32),),
        in_specs=[scalar] + [whole] * 9,
    )(place, given, signal, query, first, ends, short_filter, decays, residues, skip.reshape(1, width))
    near = lax.all_gather(gated, ("ctx", "ch"), axis_index_groups=rings(0))
    near = lax.all_gather(near, ("ctx", "ch"), axis_index_groups=rings(1)).reshape(outer, length, width)
    parts = pallas(
        mix_kernel,
        shape((inner, length, features), BF16),
        in_specs=[scalar] + [whole] * (1 + inner),
    )(place_y, near, rolled[0], *w_near)
    parts = lax.all_to_all(parts, "ch", 0, 0, axis_index_groups=along_inner)
    return pallas(sum_kernel, shape((length, features), BF16), in_specs=[whole])(parts)


def solution(mesh):
    groups = mesh.shape["ch"]
    outer = 4 if groups % 4 == 0 else 1
    in_specs = (
        P(None, "ch", "ctx"),
        P(None, "ch", None),
        P("ch", None),
        P("ch", None),
        P("ch"),
        P(None, "ch"),
    )
    return jax.shard_map(
        functools.partial(per_device, outer),
        mesh=mesh,
        in_specs=in_specs,
        out_specs=P("ctx", "ch"),
        check_vma=False,
    )
```

```python
import functools

import jax
import jax.numpy as jnp
from jax import lax
from jax.experimental import pallas as pl
from jax.experimental.pallas import tpu as pltpu
from jax.sharding import PartitionSpec as P

F32 = jnp.float32
BF16 = jnp.bfloat16
LANES = 128
SUB = 8
VMEM_LIMIT = 16 * 1024 * 1024
VMEM_WHOLE = 63 * 1024 * 1024


def pallas(body, out_shape, scratch=(), vmem=VMEM_LIMIT, **kwargs):
    return pl.pallas_call(
        body,
        out_shape=out_shape,
        scratch_shapes=list(scratch),
        compiler_params=pltpu.CompilerParams(vmem_limit_bytes=vmem),
        **kwargs,
    )


def halves(width):
    return [slice(lo, lo + LANES) for lo in range(0, width, LANES)]


def spread(row):
    return jnp.broadcast_to(row, (SUB, LANES))


def fill_line(line_ref, at, block):
    for h, cols in enumerate(halves(block.shape[1])):
        line_ref[at, h, :SUB, :] = jnp.zeros((SUB, LANES), F32)
        line_ref[at, h, SUB:, :] = block[:, cols]


def short_mix(line_ref, at, h, tap, steps):
    def rows(step):
        return line_ref[at, h, pl.ds(SUB + step, SUB, stride=steps), :]

    back2, back1 = rows(-2), rows(-1)
    for p in range(steps):
        here = rows(p)
        yield tap[0] * here + tap[1] * back1 + tap[2] * back2
        back2, back1 = back1, here


def signal_steps(k_line, v_line, filter_ref, h, cols, steps):
    chunk_id = lax.broadcasted_iota(jnp.int32, (SUB, LANES), 0)
    mixes = [
        short_mix(line_ref, at, h, [spread(filter_ref[i, m : m + 1, cols]) for m in range(3)], steps)
        for i, (line_ref, at) in enumerate((k_line, v_line), start=1)
    ]
    for p, (k, v) in enumerate(zip(*mixes)):
        signal = (k * v).astype(BF16).astype(F32)
        yield jnp.where(chunk_id == 0, 0.0, signal) if p < 2 else signal


def state_kernel(
    q_ref, k_ref, v_ref, filter_ref, decay_ref,
    sent_ref, signal_ref, query_ref, first_ref, ends_ref,
    line_ref, sums_ref,
):
    width, length = k_ref.shape[1:]
    steps = length // SUB
    modes = decay_ref.shape[0]
    blocks = [ref[0].T.astype(F32) for ref in (q_ref, k_ref, v_ref)]
    for i, block in enumerate(blocks):
        fill_line(line_ref, i, block)
    chunk_id = lax.broadcasted_iota(jnp.int32, (SUB, LANES), 0)
    from_end = float(steps) * (SUB - 1 - chunk_id).astype(F32)
    for h, cols in enumerate(halves(width)):
        rate = [spread(decay_ref[m : m + 1, cols]) for m in range(modes)]
        one_step = jnp.exp(-decay_ref[:, cols])
        keep = [spread(one_step[m : m + 1]) for m in range(modes)]
        state = [jnp.zeros((SUB, LANES), F32) for _ in range(modes)]
        pair = []
        for p, signal in enumerate(signal_steps((line_ref, 1), (line_ref, 2), filter_ref, h, cols, steps)):
            pair.append(signal)
            if p % 2:
                signal_ref[p // 2, :, cols] = jnp.concatenate(pair, axis=0).astype(BF16)
                pair = []
            state = [keep[m] * state[m] + signal for m in range(modes)]
        for m in range(modes):
            ends_ref[m, :, cols] = state[m]
            weight = jnp.exp(-rate[m] * from_end)
            sums_ref[h * modes + m : h * modes + m + 1, :] = jnp.sum(weight * state[m], axis=0, keepdims=True)
        tap = [spread(filter_ref[0, m : m + 1, cols]) for m in range(3)]
        mixes = list(short_mix(line_ref, 0, h, tap, steps))
        first_ref[0, :, cols], first_ref[1, :, cols] = mixes[:2]
        for p in range(0, steps, 2):
            query_ref[p // 2, :, cols] = jnp.concatenate(mixes[p : p + 2], axis=0).astype(BF16)
    edges = [blocks[1][-2:], blocks[2][-2:], blocks[1][:2], blocks[2][:2]]
    at = 2 * modes
    for h, cols in enumerate(halves(width)):
        for e, edge in enumerate(edges):
            for r in range(2):
                row = at + 2 * (2 * e + r) + h
                sums_ref[row : row + 1, :] = edge[r : r + 1, cols]
        sums_ref[at + 2 * SUB + 2 * h : at + 2 * SUB + 2 * h + 2, :] = blocks[0][-2:, cols]
    sums_ref[at + 2 * SUB + 4 :, :] = jnp.zeros((4, LANES), F32)
    sent = sums_ref[...].astype(BF16)
    for j in range(sent_ref.shape[0]):
        sent_ref[j] = sent


def first_signals(taps_k, taps_v, edge, last):
    def item(rows, n):
        return rows[2 * n : 2 * n + 2]

    def mixed(tap, n):
        before2, before1, here, after = item(last, n), item(last, n + 1), item(edge, n + 4), item(edge, n + 5)
        zero = tap[0] * here + tap[1] * before1 + tap[2] * before2
        one = tap[0] * after + tap[1] * here + tap[2] * before1
        return zero, one

    return [(a * b).astype(BF16).astype(F32) for a, b in zip(mixed(taps_k, 0), mixed(taps_v, 2))]


def gate_kernel(
    place_ref, given_ref, signal_ref, query_ref, first_ref, ends_ref, filter_ref, decay_ref, residue_ref, skip_ref,
    gated_ref,
    line_ref,
):
    blocks = given_ref.shape[0]
    modes, width = decay_ref.shape
    steps = 2 * signal_ref.shape[0]
    length = steps * SUB
    at = 2 * modes
    place = place_ref[0]
    chunk_id = lax.broadcasted_iota(jnp.int32, (SUB, LANES), 0)
    own = given_ref[place].astype(F32)
    before = given_ref[jnp.maximum(place - 1, 0)].astype(F32)
    before = jnp.where(place > 0, before, 0.0)
    parts = halves(width)
    rows = slice(at, at + 2 * SUB)
    both = [[jnp.concatenate([filter_ref[i, m : m + 1, cols] for cols in parts], 0) for m in range(3)] for i in (1, 2)]
    ages = [[jnp.exp(-float(length - n) * decay_ref[:, cols]) for cols in parts] for n in range(3)]
    carries = [jnp.zeros((modes, LANES), F32) for _ in parts]
    last = jnp.zeros((2 * SUB, LANES), F32)
    for j in range(blocks - 1):
        there = given_ref[j].astype(F32)
        edge = there[rows]
        zero, one = first_signals(*both, edge, last)
        for h in range(2):
            gone = there[h * modes : (h + 1) * modes] + ages[1][h] * zero[h : h + 1] + ages[2][h] * one[h : h + 1]
            carries[h] = jnp.where(j < place, ages[0][h] * carries[h] + gone, carries[h])
        last = edge
    own_first = first_signals(*both, own[rows], before[rows])
    for h, cols in enumerate(parts):
        decay = decay_ref[:, cols]
        twice = 2.0 * decay
        series = jnp.ones_like(twice)
        for n in (8, 7, 6, 5, 4, 3, 2):
            series = 1.0 - twice * (1.0 / n) * series
        weight = residue_ref[:, cols] * jnp.sqrt(twice * series)
        carry = carries[h]
        firsts = [f[h : h + 1] for f in own_first]
        tap = [filter_ref[0, m : m + 1, cols] for m in range(3)]
        q_last = before[at + 2 * SUB + 2 * h : at + 2 * SUB + 2 * h + 2]
        q_more = [tap[1] * q_last[1:2] + tap[2] * q_last[0:1], tap[2] * q_last[1:2]]
        one_step = jnp.exp(-decay)
        one_chunk = jnp.exp(-float(steps) * decay)
        chunks = {1: one_chunk, 2: one_chunk * one_chunk}
        chunks[4] = chunks[2] * chunks[2]
        aged = [jnp.exp(-float(steps - 1 - n) * decay) for n in range(2)]
        keep = [spread(one_step[m : m + 1]) for m in range(modes)]
        state = []
        for m in range(modes):
            end = ends_ref[m, :, cols]
            more = aged[0][m : m + 1] * firsts[0] + aged[1][m : m + 1] * firsts[1]
            end = jnp.where(chunk_id == 0, end + spread(more), end)
            run = jnp.where(chunk_id == 0, spread(carry[m : m + 1]), pltpu.roll(end, 1, 0))
            for far in (1, 2, 4):
                moved = jnp.where(chunk_id >= far, pltpu.roll(run, far, 0), 0.0)
                run = run + spread(chunks[far][m : m + 1]) * moved
            state.append(run)
        gain = [spread(weight[m : m + 1]) for m in range(modes)]
        skip = spread(skip_ref[0:1, cols])
        for p in range(steps):
            if p % 2 == 0:
                signals = signal_ref[p // 2, :, cols].astype(F32)
                queries = query_ref[p // 2, :, cols].astype(F32)
            signal = signals[p % 2 * SUB : (p % 2 + 1) * SUB]
            query = queries[p % 2 * SUB : (p % 2 + 1) * SUB]
            if p < 2:
                signal = jnp.where(chunk_id == 0, spread(firsts[p]), signal)
                full = (first_ref[p, :, cols] + spread(q_more[p])).astype(BF16).astype(F32)
                query = jnp.where(chunk_id == 0, full, query)
            state = [keep[m] * state[m] + signal for m in range(modes)]
            terms = [gain[m] * state[m] for m in range(modes)]
            while len(terms) > 1:
                terms = [a + b for a, b in zip(terms[::2], terms[1::2])]
            conv = terms[0].astype(BF16).astype(F32)
            line_ref[h, pl.ds(p, SUB, stride=steps), :] = query * (conv + skip * signal)
        gated_ref[:, cols] = line_ref[h].astype(BF16)


def roll_kernel(place_ref, w_ref, *refs):
    outs, sems = refs[:-1], refs[-1]
    outer, inner = w_ref.shape[:2]
    most, start = outer - 1, place_ref[1]
    copies = []
    for k, out in enumerate(outs):
        y = lax.rem(place_ref[0] + k, inner)
        copies.append(
            pltpu.make_async_copy(w_ref.at[pl.ds(start, most), y], out.at[pl.ds(0, most)], sems.at[k, 0])
        )
        copies.append(pltpu.make_async_copy(w_ref.at[lax.rem(start + most, outer), y], out.at[most], sems.at[k, 1]))
    for copy in copies:
        copy.start()
    for copy in copies:
        copy.wait()


def mix_kernel(place_ref, gated_ref, own_ref, *refs):
    w_refs, part_ref = (own_ref,) + refs[:-1], refs[-1]
    inner = part_ref.shape[0]
    for k, w_ref in enumerate(w_refs):
        part_ref[lax.rem(place_ref[0] - k + inner, inner)] = sum(
            jnp.dot(gated_ref[z], w_ref[z], preferred_element_type=F32)
            for z in range(gated_ref.shape[0])
        ).astype(BF16)


def sum_kernel(part_ref, out_ref):
    total = part_ref[0].astype(F32)
    for k in range(1, part_ref.shape[0]):
        total = total + part_ref[k].astype(F32)
    out_ref[...] = total.astype(BF16)


def per_device(outer, proj, short_filter, residues, decays, skip, w_out):
    _, width, length = proj.shape
    modes = decays.shape[1]
    features = w_out.shape[1]
    blocks = lax.axis_size("ctx")
    groups = lax.axis_size("ch")
    inner = groups // outer
    steps = length // SUB
    shape = jax.ShapeDtypeStruct

    along_inner = [[a * inner + b for b in range(inner)] for a in range(outer)]
    from_zero = ([0, 1], [2, 3]), ([0, 3], [1, 2])
    from_one = ([1, 2], [3, 0]), ([1, 0], [2, 3])
    turns = (from_one, from_zero)

    def rings(turn):
        return [
            [i * groups + a * inner + b for a in pair]
            for i in range(blocks)
            for b in range(inner)
            for pair in turns[i % 2][turn]
        ]

    odd = lax.rem(lax.axis_index("ctx"), 2)
    decays, residues = decays.T, residues.T
    short_filter = short_filter.swapaxes(1, 2)
    place = lax.axis_index("ctx").astype(jnp.int32).reshape(1)
    place_y = lax.rem(lax.axis_index("ch"), inner).astype(jnp.int32).reshape(1)
    whole = pl.BlockSpec(memory_space=pltpu.VMEM)
    scalar = pl.BlockSpec(memory_space=pltpu.SMEM)
    far = pl.BlockSpec(memory_space=pl.ANY)

    def full(*dims):
        return pl.BlockSpec(dims, lambda i: (0,) * len(dims))

    def one(i, lanes, at):
        return pl.BlockSpec((1, width, lanes), lambda g: (i, 0, at))

    sent_rows = 2 * modes + 3 * SUB
    sent, signal, query, first, ends = pallas(
        state_kernel,
        (
            shape((blocks, sent_rows, LANES), BF16),
            shape((steps // 2, 2 * SUB, width), BF16),
            shape((steps // 2, 2 * SUB, width), BF16),
            shape((2, SUB, width), F32),
            shape((modes, SUB, width), F32),
        ),
        (
            pltpu.VMEM((3, width // LANES, SUB + length, LANES), F32),
            pltpu.VMEM((sent_rows, LANES), F32),
        ),
        vmem=VMEM_WHOLE,
        grid=(1,),
        in_specs=[one(i, length, 0) for i in range(3)] + [full(3, 3, width), full(modes, width)],
        out_specs=[
            full(blocks, sent_rows, LANES),
            full(steps // 2, 2 * SUB, width),
            full(steps // 2, 2 * SUB, width),
            full(2, SUB, width),
            full(modes, SUB, width),
        ],
    )(proj, proj, proj, short_filter, decays)
    given = lax.all_to_all(sent, "ctx", 0, 0)
    w_parts = w_out.reshape(outer, inner, width, features)
    spots = jnp.stack([place_y[0], 1 - odd]).astype(jnp.int32)
    spots, sent = lax.optimization_barrier((spots, sent))
    rolled = pallas(
        roll_kernel,
        [shape((outer, width, features), BF16)] * inner,
        (pltpu.SemaphoreType.DMA((inner, 2)),),
        in_specs=[scalar, whole],
        out_specs=[whole] + [far] * (inner - 1),
    )(spots, w_parts)
    w_near = [
        lax.ppermute(
            part, "ch",
            [(a * inner + b, a * inner + (b + k + 1) % inner) for a in range(outer) for b in range(inner)],
        )
        for k, part in enumerate(rolled[1:])
    ]
    gated = pallas(
        gate_kernel,
        shape((length, width), BF16),
        (pltpu.VMEM((width // LANES, length, LANES), F32),),
        in_specs=[scalar] + [whole] * 9,
    )(place, given, signal, query, first, ends, short_filter, decays, residues, skip.reshape(1, width))
    near = lax.all_gather(gated, ("ctx", "ch"), axis_index_groups=rings(0))
    near = lax.all_gather(near, ("ctx", "ch"), axis_index_groups=rings(1)).reshape(outer, length, width)
    parts = pallas(
        mix_kernel,
        shape((inner, length, features), BF16),
        in_specs=[scalar] + [whole] * (1 + inner),
    )(place_y, near, rolled[0], *w_near)
    parts = lax.all_to_all(parts, "ch", 0, 0, axis_index_groups=along_inner)
    return pallas(sum_kernel, shape((length, features), BF16), in_specs=[whole])(parts)


def solution(mesh):
    groups = mesh.shape["ch"]
    outer = 4 if groups % 4 == 0 else 1
    in_specs = (
        P(None, "ch", "ctx"),
        P(None, "ch", None),
        P("ch", None),
        P("ch", None),
        P("ch"),
        P(None, "ch"),
    )
    return jax.shard_map(
        functools.partial(per_device, outer),
        mesh=mesh,
        in_specs=in_specs,
        out_specs=P("ctx", "ch"),
        check_vma=False,
    )
```
